32 devices in a mesh: dp: 4 (over y, x), fsdp: 8 (over z, core).
Axes of the slice: x: 2, y: 2, z: 4, core: 2. Of those that a mesh axis runs over, the one named last changes fastest.
Arguments:
- tokens: float32 [12288, 1536], P(('dp', 'fsdp')), may hold values from -6 to 6
- segment: int32 [12288], P(('dp', 'fsdp')), may hold values from 0 to 4, as said below
- timestep: int32 [128], P(('dp', 'fsdp')), may hold values from 0 to 999
- ada_weight: bfloat16 [1536, 4608], P('fsdp', 'dp'), may hold values from -0.15625 to 0.15625
- ada_bias: bfloat16 [4608], P(('dp', 'fsdp')), may hold values from -3 to 3
- in_weight: bfloat16 [1536, 6144], P('fsdp', 'dp'), may hold values from -1 to 1
- conv_weight: bfloat16 [3072, 4], P(('dp', 'fsdp')), may hold values from -3 to 3
- convolution_bias: bfloat16 [3072], P(('dp', 'fsdp')), may hold values from -3 to 3
- xproj_weight: bfloat16 [3072, 128], P(('dp', 'fsdp')), may hold values from -0.4375 to 0.4375
- dtproj_weight: bfloat16 [3072, 96], P(('dp', 'fsdp')), may hold values from -0.3125 to 0.3125
- dt_bias: bfloat16 [3072], P(('dp', 'fsdp')), may hold values from -6.1875 to -3.1875
- a_log: bfloat16 [3072, 16], P(('dp', 'fsdp')), may hold values from -3 to 0
- d_skip: bfloat16 [3072], P(('dp', 'fsdp')), may hold values from 0.5 to 1.5
- out_weight: bfloat16 [3072, 1536], P('fsdp', 'dp'), may hold values from -0.21875 to 0.21875
- cotangent: float32 [12288, 1536], P(('dp', 'fsdp')), may hold values from -6 to 6
Outputs:
- layer_out: float32 [12288, 1536], P(('dp', 'fsdp'))
- grad_tokens: float32 [12288, 1536], P(('dp', 'fsdp'))
- grad_ada_weight: float32 [1536, 4608], P('fsdp', 'dp')
- grad_ada_bias: float32 [4608], P(('dp', 'fsdp'))
- grad_in_weight: float32 [1536, 6144], P('fsdp', 'dp')
- grad_conv_weight: float32 [3072, 4], P(('dp', 'fsdp'))
- grad_conv_bias: float32 [3072], P(('dp', 'fsdp'))
- grad_xproj_weight: float32 [3072, 128], P(('dp', 'fsdp'))
- grad_dtproj_weight: float32 [3072, 96], P(('dp', 'fsdp'))
- grad_dt_bias: float32 [3072], P(('dp', 'fsdp'))
- grad_a_log: float32 [3072, 16], P(('dp', 'fsdp'))
- grad_d_skip: float32 [3072], P(('dp', 'fsdp'))
- grad_out_weight: float32 [3072, 1536], P('fsdp', 'dp')
- out_rms: float32 [], replicated
- grad_rms: float32 [], replicated
The draws below stay inside these ranges and needn't reach their ends.
Inputs may be any that keep to these rules, and one draw needn't show every extreme that they name: On each device the tokens form either one sequence of 384 tokens (segment 0 throughout) or two to 4 sequences of 96 tokens numbered 0, 1, ... in order, followed by padding marked 4; some device holds one whole sequence and some device has padding in every draw.
All inputs are finite; a program needn't handle non-finite values.
Results may differ from the reference program's by a relative error of at most 0.019.
Values may be sent and summed in bfloat16 or wider, within the bound.
No kernel may reach another device: no remote copies, remote signals or barrier semaphores. Data moves between devices by JAX's collectives and lax.ppermute only.
A program may use at most 320 MiB of HBM per device.

```python
import math
import jax
import jax.numpy as jnp
from jax import lax

D = 1536
E = 3072
N = 16
R = 96
K = 4
TOK_DEV = 384
SLOTS = 4
TOKENS = 12288
SEQS = 128


def draw_segment(key, part):
    devices = TOKENS // TOK_DEV
    kinds = jax.random.randint(key, (devices,), 0, 4)
    kinds = kinds.at[0].set(0).at[devices - 1].set(3)
    position = jnp.arange(TOK_DEV, dtype=jnp.int32)
    short_slot = position // (TOK_DEV // SLOTS)
    live_count = SLOTS + 1 - kinds
    shorts = jnp.where(short_slot[None, :] < live_count[:, None], short_slot[None, :], SLOTS)
    result = jnp.where(kinds[:, None] == 0, jnp.zeros_like(shorts), shorts)
    return result.reshape(-1).astype(jnp.int32)


def draw_in_weight(key, part):
    own_key = jax.random.fold_in(key, 11)
    base_key, common_key = jax.random.split(own_key)
    deviation = 1.0 / jnp.sqrt(jnp.float32(D))
    base = jnp.clip(jax.random.normal(base_key, (D, 2 * E), jnp.float32), -6.0, 6.0) * deviation
    common = jnp.clip(jax.random.normal(common_key, (2 * E,), jnp.float32), -4.0, 4.0) * (0.7 * deviation)
    return (base + common[None, :]).astype(jnp.bfloat16)


def set_ends(values, rng, low, top_value):
    shape = values.shape
    spot = [jax.random.randint(jax.random.fold_in(rng, axis), (), 0, shape[axis]) for axis in range(len(shape))]
    values = values.at[tuple(spot)].set(low)
    longest = shape.index(max(shape))
    spot[longest] = (spot[longest] + 1) % shape[longest]
    return values.at[tuple(spot)].set(top_value)


def levels(stream_key, extent, shards, low, top_value):
    gain, own = 1.0, jax.random.fold_in(stream_key, 6)
    for dim, parts in shards:
        draws = jnp.exp(jax.random.uniform(jax.random.fold_in(own, dim), (parts,), jnp.float32, low / len(shards), top_value / len(shards)))
        gain = gain * jnp.repeat(draws, extent[dim] // parts).reshape([-1 if axis == dim else 1 for axis in range(len(extent))])
    return gain


def gaussian(stream_key, extent, scale, most, cuts=(), kind=jnp.bfloat16):
    array = jax.random.normal(stream_key, extent, jnp.float32) * scale
    if len(cuts) > 0:
        array = levels(stream_key, extent, cuts, -0.22, 0.18) * array
    return jnp.clip(array, min=-most, max=most).astype(kind)


def setup_inputs(seed: int = 0) -> dict:
    key_list = jax.random.split(jax.random.key(seed), 16)
    return {
        "tokens": gaussian(key_list[0], (TOKENS, D), 1.0, 6.0, ((0, 32),), jnp.float32),
        "segment": draw_segment(jax.random.fold_in(key_list[15], 71), 0),
        "timestep": set_ends(jax.random.randint(key_list[2], (SEQS,), 0, 1000), jax.random.fold_in(key_list[2], 1), 0, 999).astype(jnp.int32),
        "ada_weight": gaussian(key_list[3], (D, 3 * D), D ** -0.5, 0.15625, ((0, 8), (1, 4))),
        "ada_bias": gaussian(key_list[4], (3 * D,), 0.5, 3.0, ((0, 32),)),
        "in_weight": draw_in_weight(jax.random.fold_in(key_list[15], 71), 0),
        "conv_weight": gaussian(key_list[6], (E, K), 0.5, 3.0, ((0, 32),)),
        "convolution_bias": gaussian(key_list[7], (E,), 0.3, 3.0, ((0, 32),)),
        "xproj_weight": gaussian(key_list[8], (E, R + 2 * N), (E // 16) ** -0.5, 0.4375, ((0, 32),)),
        "dtproj_weight": gaussian(key_list[9], (E, R), 0.02, 0.3125, ((0, 32),)),
        "dt_bias": jnp.clip(-6.1875 + 3.0 * jax.random.uniform(key_list[10], (E,), jnp.float32) ** levels(key_list[10], (E,), ((0, 32),), -0.2, 0.2), -6.1875, -3.1875).astype(jnp.bfloat16),
        "a_log": jnp.clip(-3.0 + 3.0 * jax.random.uniform(key_list[11], (E, N), jnp.float32) ** levels(key_list[11], (E, N), ((0, 32),), -0.2, 0.2), -3.0, 0.0).astype(jnp.bfloat16),
        "d_skip": jnp.clip(0.5 + 1.0 * jax.random.uniform(key_list[12], (E,), jnp.float32) ** levels(key_list[12], (E,), ((0, 32),), -0.2, 0.2), 0.5, 1.5).astype(jnp.bfloat16),
        "out_weight": gaussian(key_list[13], (E, D), (E // 4) ** -0.5, 0.21875, ((0, 8), (1, 4))),
        "cotangent": gaussian(key_list[14], (TOKENS, D), 1.0, 6.0, ((0, 32),), jnp.float32),
    }


maximal_precision = lax.Precision.HIGHEST

@jax.custom_vjp
def low(v):
    return lax.optimization_barrier(v.astype(jnp.bfloat16)).astype(jnp.float32)

@jax.custom_vjp
def low_back(v):
    return v

def low_keep(v):
    return (low(v), None)

def low_pass(kept, grad):
    return (grad,)

def back_keep(v):
    return (v, None)

def back_low(kept, grad):
    return (low(grad),)
low.defvjp(low_keep, low_pass)
low_back.defvjp(back_keep, back_low)

def embed_columns(time_values, first_column, column_count, model_width):
    half_width = model_width // 2
    column = first_column + jnp.arange(column_count, dtype=jnp.int32)
    lower_half = column < half_width
    freq_index = jnp.where(lower_half, column, column - half_width).astype(jnp.float32)
    frequency = jnp.exp(freq_index * (-math.log(10000.0) / half_width))
    angles = time_values.astype(jnp.float32)[:, None] * frequency[None, :]
    return jax.nn.silu(jnp.where(lower_half[None, :], jnp.cos(angles), jnp.sin(angles)))

def conv_series(values, segment, conv_w, conv_b, direction):
    length = values.shape[0]
    taps = conv_w.shape[1]
    result = conv_b[None, :] + conv_w[:, taps - 1][None, :] * values
    for offset in range(1, taps):
        zero_rows = jnp.zeros((offset, values.shape[1]), values.dtype)
        edge_seg = jnp.full((offset,), -1, jnp.int32)
        if direction > 0:
            moved = jnp.concatenate([zero_rows, values[:length - offset]], axis=0)
            moved_seg = jnp.concatenate([edge_seg, segment[:length - offset].astype(jnp.int32)])
        else:
            moved = jnp.concatenate([values[offset:], zero_rows], axis=0)
            moved_seg = jnp.concatenate([segment[offset:].astype(jnp.int32), edge_seg])
        matched = (moved_seg == segment).astype(values.dtype)[:, None]
        result = result + conv_w[:, taps - 1 - offset][None, :] * moved * matched
    return result

def chain_reference(series, step_size, b_rows, c_rows, keep_mask, decay, backward):

    def step_forward(state, slices):
        u_now, d_now, b_now, c_now, k_now = slices
        state = jnp.exp(d_now[:, None] * decay) * state * k_now + (d_now * u_now)[:, None] * b_now[None, :]
        return (state, lax.optimization_barrier(jnp.sum(state * c_now[None, :], axis=1)))
    _, outputs = lax.scan(step_forward, jnp.zeros((E, N), jnp.float32), (series, step_size, b_rows, c_rows, keep_mask), reverse=backward)
    return outputs

def mixer(inner_pair, segment, conv_w, conv_b, x_proj, dt_proj, bias_dt, a_log, d_skip):
    x_part = inner_pair[:, :E]
    z_part = inner_pair[:, E:]
    decay = -jnp.exp(a_log)
    edge_seg = jnp.full((1,), -1, jnp.int32)
    preceding_value = jnp.concatenate([edge_seg, segment[:-1].astype(jnp.int32)])
    after = jnp.concatenate([segment[1:].astype(jnp.int32), edge_seg])
    total = jnp.zeros((inner_pair.shape[0], E), jnp.float32)
    for direction in (1, -1):
        series = jax.nn.silu(conv_series(x_part, segment, conv_w, conv_b, direction))
        projected = jnp.dot(series, x_proj, precision=maximal_precision)
        step_size = jax.nn.softplus(jnp.dot(projected[:, :R], dt_proj.T, precision=maximal_precision) + bias_dt[None, :])
        b_rows = projected[:, R:R + N]
        c_rows = projected[:, R + N:]
        neighbour = preceding_value if direction > 0 else after
        keep_mask = (neighbour == segment).astype(jnp.float32)
        scanned = chain_reference(series, step_size, b_rows, c_rows, keep_mask, decay, direction < 0)
        total = total + scanned + d_skip[None, :] * series
    return total * jax.nn.silu(z_part)

def row_forward(params, row_tokens, row_segment, row_times):
    ada_w, ada_b, in_w, conv_w, conv_b, x_proj, dt_proj, bias_dt, a_log, d_skip, out_w = params
    condition = low(embed_columns(row_times, 0, D, D))
    modulation = low_back(jnp.dot(condition, ada_w, precision=maximal_precision) + ada_b[None, :])
    picker = (row_segment[:, None] == jnp.arange(SLOTS, dtype=jnp.int32)[None, :]).astype(jnp.float32)
    per_token = jnp.dot(picker, modulation, precision=maximal_precision)
    shift_mod = per_token[:, :D]
    scale_mod = per_token[:, D:2 * D]
    gate_mod = per_token[:, 2 * D:]
    centered = row_tokens - lax.optimization_barrier(jnp.mean(row_tokens, axis=1, keepdims=True))
    inv_std = lax.rsqrt(lax.optimization_barrier(jnp.mean(centered * centered, axis=1, keepdims=True)) + 1e-06)
    normed = centered * inv_std
    hidden = low(normed * (1.0 + scale_mod) + shift_mod)
    inner_pair = low_back(jnp.dot(hidden, in_w, precision=maximal_precision))
    mixer_out = low(mixer(inner_pair, row_segment, conv_w, conv_b, x_proj, dt_proj, bias_dt, a_log, d_skip))
    branch = low_back(jnp.dot(mixer_out, out_w, precision=maximal_precision))
    return row_tokens + gate_mod * branch

def reference(tokens, segment, timestep, ada_weight, ada_bias, in_weight, conv_weight, convolution_bias, xproj_weight, dtproj_weight, dt_bias, a_log, d_skip, out_weight, cotangent):
    params = tuple((member.astype(jnp.float32) for member in (ada_weight, ada_bias, in_weight, conv_weight, convolution_bias, xproj_weight, dtproj_weight, dt_bias, a_log, d_skip, out_weight)))
    segment_rows = segment.reshape(-1, TOK_DEV)
    time_rows = timestep.reshape(-1, SLOTS)

    def whole(params_in, tokens_in):

        def one_row(slices):
            return jax.checkpoint(row_forward)(params_in, slices[0], slices[1], slices[2])
        return lax.map(one_row, (tokens_in.reshape(-1, TOK_DEV, D), segment_rows, time_rows))
    outputs, pullback = jax.vjp(whole, params, tokens)
    param_grads, token_grads = pullback(cotangent.reshape(-1, TOK_DEV, D))
    layer_out = outputs.reshape(-1, D)
    grad_tokens = token_grads.reshape(-1, D)
    valid = (segment < SLOTS).astype(jnp.float32)[:, None]
    counted = jnp.sum(valid) * D
    out_rms = jnp.sqrt(jnp.sum(layer_out * layer_out * valid) / counted)
    grad_rms = jnp.sqrt(jnp.sum(grad_tokens * grad_tokens * valid) / counted)
    return (layer_out, grad_tokens, param_grads[0], param_grads[1], param_grads[2], param_grads[3], param_grads[4], param_grads[5], param_grads[6], param_grads[7], param_grads[8], param_grads[9], param_grads[10], out_rms, grad_rms)
```

```python
import math

import jax
import jax.numpy as jnp
from jax import lax
from jax.experimental import pallas as pl
from jax.experimental.pallas import tpu as pltpu
from jax.sharding import PartitionSpec as P

F32 = jnp.float32
BF16 = jnp.bfloat16
LN2 = math.log(2.0)
BOTH = ("dp", "fsdp")
high = lax.Precision.HIGHEST
GROUP = 4


def embed_columns(time_values, column, model_width):
    half_width = model_width // 2
    lower_half = column < half_width
    freq_index = jnp.where(lower_half, column, column - half_width).astype(F32)
    frequency = jnp.exp(freq_index * (-math.log(10000.0) / half_width))
    angles = time_values.astype(F32)[:, None] * frequency[None, :]
    return jax.nn.silu(jnp.where(lower_half[None, :], jnp.cos(angles), jnp.sin(angles)))


def to_rows(v):
    t, e = v.shape
    return v.reshape(t // 8, 8, e // 128, 128).transpose(0, 2, 1, 3).reshape(t * e // 128, 128)


def from_rows(r, t, e):
    return r.reshape(t // 8, e // 128, 8, 128).transpose(0, 2, 1, 3).reshape(t, e)


def fill_columns(proj_ref, bc_ref, tokens, first, group, states):
    def fill(i, _):
        p = proj_ref[pl.ds(pl.multiple_of(i * 8, 8), 8), :]
        for s in range(2):
            for n in range(GROUP):
                col = first + s * states + group * GROUP + n
                row = pl.multiple_of((s * GROUP + n) * tokens + i * 8, 8)
                bc_ref[pl.ds(row, 8), :] = jnp.broadcast_to(p[:, col : col + 1], (8, 128))
        return 0

    lax.fori_loop(0, tokens // 8, fill, 0)


def scan_forward(keep, proj, step, series, decay2, *, rev, tokens, inner, states, rank):
    blocks, tiles, octets = inner // 1024, inner // 128, tokens // 8

    def body(keep_ref, proj_ref, d_ref, u_ref, a_ref, y_ref, bc_ref):
        for ng in range(states // GROUP):
            fill_columns(proj_ref, bc_ref, tokens, rank, ng, states)
            a = [
                [a_ref[pl.ds((ng * GROUP + n) * tiles + c * 8, 8), :] for c in range(blocks)]
                for n in range(GROUP)
            ]

            def octet(i, hs):
                g = (octets - 1 - i) if rev else i
                keep_now = keep_ref[i]
                hs = [h * keep_now for h in hs]
                base = pl.multiple_of(g * (tiles * 8), 8)
                for j in range(8):
                    tt = 7 - j if rev else j
                    t = g * 8 + tt
                    for c in range(blocks):
                        sl = pl.ds(base + c * 64 + tt, 8, stride=8)
                        d = d_ref[sl, :]
                        du = d * u_ref[sl, :]
                        acc = None
                        for n in range(GROUP):
                            b = bc_ref[pl.ds(n * tokens + t, 1), :]
                            cc = bc_ref[pl.ds((GROUP + n) * tokens + t, 1), :]
                            k = n * blocks + c
                            hs[k] = jnp.exp2(d * a[n][c]) * hs[k] + du * b
                            acc = hs[k] * cc if acc is None else acc + hs[k] * cc
                        if ng == 0:
                            y_ref[sl, :] = acc
                        else:
                            y_ref[sl, :] = y_ref[sl, :] + acc
                return hs

            lax.fori_loop(0, octets, octet, [jnp.zeros((8, 128), F32)] * (GROUP * blocks))

    vmem = pl.BlockSpec(memory_space=pltpu.VMEM)
    return pl.pallas_call(
        body,
        out_shape=jax.ShapeDtypeStruct((tokens * tiles, 128), F32),
        in_specs=[pl.BlockSpec(memory_space=pltpu.SMEM)] + [vmem] * 4,
        out_specs=vmem,
        scratch_shapes=[pltpu.VMEM((2 * GROUP * tokens, 128), F32)],
        compiler_params=pltpu.CompilerParams(vmem_limit_bytes=56 << 20),
        cost_estimate=pl.CostEstimate(
            flops=tokens * inner * states * 7,
            bytes_accessed=3 * tokens * inner * 4,
            transcendentals=tokens * inner * states,
        ),
        name="scan_forward",
    )(keep, proj, step, series, decay2)


def scan_backward(keep, proj, step, series, grad, decay2, *, rev, tokens, inner, states, rank):
    blocks, tiles, octets = inner // 1024, inner // 128, tokens // 8
    slots = GROUP * blocks

    def body(
        keep_ref, proj_ref, d_ref, u_ref, g_ref, a_ref, ddu_ref, dd_ref, r_ref, da_ref, bc_ref, h_ref, q_ref
    ):
        zero = jnp.zeros((8, 128), F32)
        for ng in range(states // GROUP):
            fill_columns(proj_ref, bc_ref, tokens, rank, ng, states)
            a = [
                [a_ref[pl.ds((ng * GROUP + n) * tiles + c * 8, 8), :] for c in range(blocks)]
                for n in range(GROUP)
            ]
            for k in range(slots):
                h_ref[pl.ds(k * 8, 8), :] = zero

            def ahead(i, hs):
                g = (octets - 1 - i) if rev else i
                keep_now = keep_ref[i]
                hs = [h * keep_now for h in hs]
                base = pl.multiple_of(g * (tiles * 8), 8)
                for j in range(8):
                    tt = 7 - j if rev else j
                    t = g * 8 + tt
                    hb = pl.multiple_of((i * 8 + j + 1) * (slots * 8), 8)
                    for c in range(blocks):
                        sl = pl.ds(base + c * 64 + tt, 8, stride=8)
                        d = d_ref[sl, :]
                        du = d * u_ref[sl, :]
                        for n in range(GROUP):
                            b = bc_ref[pl.ds(n * tokens + t, 1), :]
                            k = n * blocks + c
                            hs[k] = jnp.exp2(d * a[n][c]) * hs[k] + du * b
                            h_ref[pl.ds(hb + k * 8, 8), :] = hs[k]
                return hs

            lax.fori_loop(0, octets, ahead, [zero] * slots)

            def back(ii, carry):
                gs, das = [list(v) for v in carry]
                i = octets - 1 - ii
                g = (octets - 1 - i) if rev else i
                keep_now = keep_ref[i]
                base = pl.multiple_of(g * (tiles * 8), 8)
                for jj in range(8):
                    j = 7 - jj
                    tt = 7 - j if rev else j
                    t = g * 8 + tt
                    hb = pl.multiple_of((i * 8 + j) * (slots * 8), 8)
                    pb, pc = [None] * GROUP, [None] * GROUP
                    for c in range(blocks):
                        sl = pl.ds(base + c * 64 + tt, 8, stride=8)
                        d = d_ref[sl, :]
                        du = d * u_ref[sl, :]
                        gy = g_ref[sl, :]
                        ddu = dd = None
                        for n in range(GROUP):
                            b = bc_ref[pl.ds(n * tokens + t, 1), :]
                            cc = bc_ref[pl.ds((GROUP + n) * tokens + t, 1), :]
                            k = n * blocks + c
                            before = h_ref[pl.ds(hb + k * 8, 8), :]
                            after = h_ref[pl.ds(hb + (slots + k) * 8, 8), :]
                            adj = gs[k] + cc * gy
                            x = after * gy
                            pc[n] = x if c == 0 else pc[n] + x
                            x = adj * du
                            pb[n] = x if c == 0 else pb[n] + x
                            x = adj * b
                            ddu = x if n == 0 else ddu + x
                            moved = adj * jnp.exp2(d * a[n][c])
                            if j == 0:
                                moved = moved * keep_now
                            gs[k] = moved
                            m = moved * before
                            x = m * a[n][c]
                            dd = x if n == 0 else dd + x
                            das[k] = das[k] + m * d
                        if ng == 0:
                            ddu_ref[sl, :] = ddu
                            dd_ref[sl, :] = dd
                        else:
                            ddu_ref[sl, :] = ddu_ref[sl, :] + ddu
                            dd_ref[sl, :] = dd_ref[sl, :] + dd
                    for n in range(GROUP):
                        q_ref[pl.ds(j * 64 + n * 8, 8), :] = pb[n]
                        q_ref[pl.ds(j * 64 + (GROUP + n) * 8, 8), :] = pc[n]
                for j in range(8):
                    tt = 7 - j if rev else j
                    t = g * 8 + tt
                    s = None
                    for q in range(8):
                        x = q_ref[pl.ds(j * 64 + q, 8, stride=8), :]
                        s = x if s is None else s + x
                    r_ref[pl.ds(pl.multiple_of((ng * tokens + t) * 8, 8), 8), :] = s
                return gs, das

            _, das = lax.fori_loop(0, octets, back, ([zero] * slots, [zero] * slots))
            for n in range(GROUP):
                for c in range(blocks):
                    da_ref[pl.ds((ng * GROUP + n) * tiles + c * 8, 8), :] = das[n * blocks + c]

    vmem = pl.BlockSpec(memory_space=pltpu.VMEM)
    rows = tokens * tiles
    return pl.pallas_call(
        body,
        out_shape=(
            jax.ShapeDtypeStruct((rows, 128), F32),
            jax.ShapeDtypeStruct((rows, 128), F32),
            jax.ShapeDtypeStruct((states // GROUP * tokens * 8, 128), F32),
            jax.ShapeDtypeStruct((states * tiles, 128), F32),
        ),
        in_specs=[pl.BlockSpec(memory_space=pltpu.SMEM)] + [vmem] * 5,
        out_specs=(vmem,) * 4,
        scratch_shapes=[
            pltpu.VMEM((2 * GROUP * tokens, 128), F32),
            pltpu.VMEM((slots * 8 * (tokens + 1), 128), F32),
            pltpu.VMEM((512, 128), F32),
        ],
        compiler_params=pltpu.CompilerParams(vmem_limit_bytes=60 << 20),
        cost_estimate=pl.CostEstimate(
            flops=tokens * inner * states * 20,
            bytes_accessed=5 * tokens * inner * 4,
            transcendentals=2 * tokens * inner * states,
        ),
        name="scan_backward",
    )(keep, proj, step, series, grad, decay2)


def conv_pair(values, segment, conv_w, conv_b):
    length, taps = values.shape[0], conv_w.shape[1]
    results = []
    for direction in (1, -1):
        result = conv_b[None, :] + conv_w[:, taps - 1][None, :] * values
        for offset in range(1, taps):
            zero_rows = jnp.zeros((offset, values.shape[1]), values.dtype)
            edge_seg = jnp.full((offset,), -1, jnp.int32)
            if direction > 0:
                moved = jnp.concatenate([zero_rows, values[: length - offset]], axis=0)
                moved_seg = jnp.concatenate([edge_seg, segment[: length - offset]])
            else:
                moved = jnp.concatenate([values[offset:], zero_rows], axis=0)
                moved_seg = jnp.concatenate([segment[offset:], edge_seg])
            matched = (moved_seg == segment).astype(values.dtype)[:, None]
            result = result + conv_w[:, taps - 1 - offset][None, :] * moved * matched
        results.append(jax.nn.silu(result))
    return tuple(results)


def per_device(
    tokens,
    segment,
    timestep,
    ada_weight,
    ada_bias,
    in_weight,
    conv_weight,
    convolution_bias,
    xproj_weight,
    dtproj_weight,
    dt_bias,
    a_log,
    d_skip,
    out_weight,
    cotangent,
):
    dp, fsdp = lax.axis_size("dp"), lax.axis_size("fsdp")
    devices = dp * fsdp
    slots = timestep.shape[0]
    length, width = tokens.shape
    taps, rank, states = conv_weight.shape[1], dtproj_weight.shape[1], a_log.shape[1]
    own = conv_weight.shape[0]
    inner = own * devices
    contract_rows = (((0,), (0,)), ((), ()))
    contract_cols = (((1,), (1,)), ((), ()))

    def full(w):
        return lax.all_gather(
            lax.all_gather(w, "dp", axis=1, tiled=True), "fsdp", axis=0, tiled=True
        )

    parts = [
        xproj_weight,
        dtproj_weight,
        conv_weight,
        convolution_bias[:, None],
        dt_bias[:, None],
        d_skip[:, None],
        a_log,
    ]
    widths = [p.shape[1] for p in parts]
    total_width = -(-sum(widths) // 128) * 128
    packed = jnp.concatenate(parts, axis=1)
    packed = jnp.pad(packed, ((0, 0), (0, total_width - packed.shape[1])))
    packed = lax.all_gather(packed, BOTH, axis=0, tiled=True).astype(F32)
    pieces, at = [], 0
    for w in widths:
        pieces.append(packed[:, at : at + w])
        at += w
    x_proj, dt_proj, conv_w, conv_b, bias_dt, skip, alog = pieces
    conv_b, bias_dt, skip = conv_b[:, 0], bias_dt[:, 0], skip[:, 0]

    times = lax.all_gather(timestep, BOTH, axis=0, tiled=True)
    ada_rows, ada_cols = ada_weight.shape
    row0 = lax.axis_index("fsdp") * ada_rows
    condition = embed_columns(
        times, row0 + jnp.arange(ada_rows, dtype=jnp.int32), width
    ).astype(BF16)
    bias_cols = ada_bias.shape[0]
    bias_part = lax.dynamic_update_slice(
        jnp.zeros((ada_cols,), F32), ada_bias.astype(F32), (lax.axis_index("fsdp") * bias_cols,)
    )
    partial = jnp.dot(condition, ada_weight, preferred_element_type=F32) + bias_part[None, :]
    swapped = lax.all_to_all(partial, BOTH, 0, 0, tiled=True)
    modulation = (
        swapped.reshape(dp, fsdp, slots, ada_cols).sum(axis=1).transpose(1, 0, 2).reshape(slots, dp * ada_cols)
    )
    picker = (segment[:, None] == jnp.arange(slots, dtype=jnp.int32)[None, :]).astype(F32)
    per_token = jnp.dot(picker, modulation, precision=high)
    shift_mod = per_token[:, :width]
    scale_mod = per_token[:, width : 2 * width]
    gate_mod = per_token[:, 2 * width :]
    centered = tokens - jnp.mean(tokens, axis=1, keepdims=True)
    inv_std = lax.rsqrt(jnp.mean(centered * centered, axis=1, keepdims=True) + 1e-06)
    normed = centered * inv_std
    hidden = (normed * (1.0 + scale_mod) + shift_mod).astype(BF16)

    in_full = full(in_weight)
    x_part = jnp.dot(hidden, in_full[:, :inner], preferred_element_type=F32)
    z_part = jnp.dot(hidden, in_full[:, inner:], preferred_element_type=F32)

    same = (segment[1:] == segment[:-1]).astype(F32)
    same = jnp.concatenate([jnp.zeros((1,), F32), same, jnp.zeros((1,), F32)])
    keeps = (same[0:length:8], same[8 : length + 1 : 8][::-1])

    decay = -jnp.exp(alog)
    decay2 = (decay * (1.0 / LN2)).T.reshape(states * inner // 128, 128)
    sizes = dict(tokens=length, inner=inner, states=states, rank=rank)

    series, conv_pull = jax.vjp(
        lambda v, w, b: conv_pair(v, segment, w, b), x_part, conv_w, conv_b
    )
    proj, step = [], []
    total = skip[None, :] * (series[0] + series[1])
    for k in range(2):
        projected = jnp.dot(series[k], x_proj, precision=high)
        pre = jnp.dot(projected[:, :rank], dt_proj.T, precision=high) + bias_dt[None, :]
        proj.append(projected)
        step.append(jax.nn.softplus(pre))
        scanned = scan_forward(
            keeps[k], projected, to_rows(step[k]), to_rows(series[k]), decay2, rev=k == 1, **sizes
        )
        total = total + from_rows(scanned, length, inner)

    gate = jax.nn.sigmoid(z_part)
    silu_z = z_part * gate
    mixer_low = (total * silu_z).astype(BF16)
    out_full = full(out_weight)
    branch = jnp.dot(mixer_low, out_full, preferred_element_type=F32)
    layer_out = tokens + gate_mod * branch

    branch_grad = (cotangent * gate_mod).astype(BF16)
    gate_grad = cotangent * branch
    grad_out_w = lax.dot_general(
        mixer_low, branch_grad, contract_rows, preferred_element_type=F32
    ).astype(BF16)
    mixer_grad = lax.dot_general(branch_grad, out_full, contract_cols, preferred_element_type=F32)
    total_grad = mixer_grad * silu_z
    z_grad = (mixer_grad * total * (gate * (1.0 + z_part * (1.0 - gate)))).astype(BF16)

    series_grad = []
    xproj_grad = dtproj_grad = bias_grad = alog_grad = 0.0
    for k in range(2):
        ddu, dd, r, da = scan_backward(
            keeps[k],
            proj[k],
            to_rows(step[k]),
            to_rows(series[k]),
            to_rows(total_grad),
            decay2,
            rev=k == 1,
            **sizes,
        )
        ddu, dd = from_rows(ddu, length, inner), from_rows(dd, length, inner)
        bc_grad = (
            jnp.sum(r, axis=-1)
            .reshape(states // GROUP, length, 2, GROUP)
            .transpose(1, 2, 0, 3)
            .reshape(length, 2 * states)
        )
        step_grad = ddu * series[k] + LN2 * dd
        pre_grad = step_grad * (1.0 - jnp.exp(-step[k]))
        proj_grad = jnp.concatenate([jnp.dot(pre_grad, dt_proj, precision=high), bc_grad], axis=1)
        series_grad.append(
            ddu * step[k]
            + skip[None, :] * total_grad
            + lax.dot_general(proj_grad, x_proj, contract_cols, precision=high)
        )
        xproj_grad += lax.dot_general(series[k], proj_grad, contract_rows, precision=high)
        dtproj_grad += lax.dot_general(pre_grad, proj[k][:, :rank], contract_rows, precision=high)
        bias_grad += jnp.sum(pre_grad, axis=0)
        alog_grad += da
    alog_grad = alog_grad.reshape(states, inner).T * decay
    skip_grad = jnp.sum(total_grad * (series[0] + series[1]), axis=0)
    x_grad, conv_w_grad, conv_b_grad = conv_pull(tuple(series_grad))
    x_grad = x_grad.astype(BF16)
    pair_low = jnp.concatenate([x_grad, z_grad], axis=1)

    grad_in_w = lax.dot_general(hidden, pair_low, contract_rows, preferred_element_type=F32).astype(BF16)
    hidden_grad = lax.dot_general(pair_low, in_full, contract_cols, preferred_element_type=F32)
    normed_grad = hidden_grad * (1.0 + scale_mod)
    grad_tokens = cotangent + inv_std * (
        normed_grad
        - jnp.mean(normed_grad, axis=1, keepdims=True)
        - normed * jnp.mean(normed_grad * normed, axis=1, keepdims=True)
    )
    token_mod_grad = jnp.concatenate([hidden_grad, hidden_grad * normed, gate_grad], axis=1)
    mod_low = lax.dot_general(picker, token_mod_grad, contract_rows, precision=high).astype(BF16)
    mod_all = lax.all_gather(mod_low, BOTH, axis=0, tiled=True)
    mod_cols = lax.dynamic_slice_in_dim(mod_all, lax.axis_index("dp") * ada_cols, ada_cols, axis=1)
    grad_ada_w = lax.dot_general(condition, mod_cols, contract_rows, preferred_element_type=F32)
    grad_ada_b = jnp.sum(
        lax.dynamic_slice_in_dim(
            mod_cols, lax.axis_index("fsdp") * bias_cols, bias_cols, axis=1
        ).astype(F32),
        axis=0,
    )

    def scattered(g):
        rows = lax.psum_scatter(g, "fsdp", scatter_dimension=0, tiled=True)
        return lax.psum_scatter(rows, "dp", scatter_dimension=1, tiled=True).astype(F32)

    grad_in_shard = scattered(grad_in_w)
    grad_out_shard = scattered(grad_out_w)
    small = jnp.concatenate(
        [
            xproj_grad,
            dtproj_grad,
            conv_w_grad,
            conv_b_grad[:, None],
            bias_grad[:, None],
            skip_grad[:, None],
            alog_grad,
        ],
        axis=1,
    )
    small = jnp.pad(small, ((0, 0), (0, total_width - small.shape[1])))
    small = lax.psum_scatter(small, BOTH, scatter_dimension=0, tiled=True)
    pieces, at = [], 0
    for w in widths:
        pieces.append(small[:, at : at + w])
        at += w
    g_xproj, g_dtproj, g_conv_w, g_conv_b, g_bias, g_skip, g_alog = pieces

    valid = (segment < slots).astype(F32)[:, None]
    out_sq, grad_sq, counted = lax.psum(
        (
            jnp.sum(layer_out * layer_out * valid),
            jnp.sum(grad_tokens * grad_tokens * valid),
            jnp.sum(valid) * width,
        ),
        BOTH,
    )
    return (
        layer_out,
        grad_tokens,
        grad_ada_w,
        grad_ada_b,
        grad_in_shard,
        g_conv_w,
        g_conv_b[:, 0],
        g_xproj,
        g_dtproj,
        g_bias[:, 0],
        g_alog,
        g_skip[:, 0],
        grad_out_shard,
        jnp.sqrt(out_sq / counted),
        jnp.sqrt(grad_sq / counted),
    )


def solution(mesh):
    rows, flat, block = P(BOTH, None), P(BOTH), P("fsdp", "dp")
    return jax.shard_map(
        per_device,
        mesh=mesh,
        in_specs=(
            rows, flat, flat, block, flat, block, rows, flat, rows, rows, flat, rows, flat, block, rows,
        ),
        out_specs=(
            rows, rows, block, flat, block, rows, flat, rows, rows, flat, rows, flat, block, P(), P(),
        ),
        check_vma=False,
    )
```

```python
import math

import jax
import jax.numpy as jnp
from jax import lax
from jax.experimental import pallas as pl
from jax.experimental.pallas import tpu as pltpu
from jax.sharding import Mesh, PartitionSpec as P

F32 = jnp.float32
BF16 = jnp.bfloat16
LN2 = math.log(2.0)
ALL = ("dp", "fz", "core")
high = lax.Precision.HIGHEST
GROUP = 4


def embed_columns(time_values, column, model_width):
    half_width = model_width // 2
    lower_half = column < half_width
    freq_index = jnp.where(lower_half, column, column - half_width).astype(F32)
    frequency = jnp.exp(freq_index * (-math.log(10000.0) / half_width))
    angles = time_values.astype(F32)[:, None] * frequency[None, :]
    return jax.nn.silu(jnp.where(lower_half[None, :], jnp.cos(angles), jnp.sin(angles)))


def fill_columns(proj_ref, bc_ref, tokens, first, group, states):
    def fill(i, _):
        p = proj_ref[pl.ds(pl.multiple_of(i * 8, 8), 8), :]
        for s in range(2):
            for n in range(GROUP):
                col = first + s * states + group * GROUP + n
                row = pl.multiple_of((s * GROUP + n) * tokens + i * 8, 8)
                bc_ref[pl.ds(row, 8), :] = jnp.broadcast_to(p[:, col : col + 1], (8, 128))
        return 0

    lax.fori_loop(0, tokens // 8, fill, 0)


VMEM = pl.BlockSpec(memory_space=pltpu.VMEM)
SMEM = pl.BlockSpec(memory_space=pltpu.SMEM)
ANY = pl.BlockSpec(memory_space=pl.ANY)


def dot(a, b):
    return jnp.dot(a, b, preferred_element_type=F32)


def dot_nt(a, b):
    return lax.dot_general(a, b, (((1,), (1,)), ((), ())), preferred_element_type=F32)


def shifted(ext, j, ahead):
    n = ext.shape[0] - 2
    sub = lax.broadcasted_iota(jnp.int32, (n, 8, 128), 1)
    if ahead:
        r = pltpu.roll(ext, 8 - j, 1)
        return jnp.where(sub >= 8 - j, r[2:], r[1:-1])
    r = pltpu.roll(ext, j, 1)
    return jnp.where(sub < j, r[:-2], r[1:-1])


def extended(ref, k, q, size, keep_ref, slots):
    zero = jnp.zeros((1, 8, 128), F32)
    lo, hi = q * size, (q + 1) * size
    before = ref[pl.ds(lo - 1, 1), k] * keep_ref[q] if q else zero
    after = ref[pl.ds(hi, 1), k] * keep_ref[q + 1] if q < slots - 1 else zero
    return jnp.concatenate([before, ref[pl.ds(lo, size), k], after], axis=0)


def convolved(ext, p, taps):
    here = ext[1:-1]
    both, moves = [], []
    for ahead in (False, True):
        c = p[taps : taps + 1][None] + p[taps - 1 : taps][None] * here
        for j in range(1, taps):
            m = shifted(ext, j, ahead)
            moves.append(m)
            c = c + p[taps - 1 - j : taps - j][None] * m
        both.append(c)
    return both, moves


def project(hidden, weight, *, rows, length, inner):
    blocks, owners, _, cols = weight.shape
    tiles = cols // 128

    def body(h_ref, w_ref, o_ref):
        w = w_ref[0].reshape(owners * rows, cols)
        r = dot(h_ref[...], w)
        for k in range(tiles):
            o_ref[:, k] = r[:, k * 128 : (k + 1) * 128].reshape(length // 8, 8, 128)

    return pl.pallas_call(
        body,
        grid=(blocks,),
        out_shape=jax.ShapeDtypeStruct((length // 8, inner // 128, 8, 128), F32),
        in_specs=[
            pl.BlockSpec(hidden.shape, lambda b: (0, 0)),
            pl.BlockSpec((1, owners, rows, cols), lambda b: (b, 0, 0, 0)),
        ],
        out_specs=pl.BlockSpec((length // 8, tiles, 8, 128), lambda b: (0, b, 0, 0)),
        compiler_params=pltpu.CompilerParams(vmem_limit_bytes=40 << 20),
        cost_estimate=pl.CostEstimate(
            flops=2 * length * hidden.shape[1] * inner,
            bytes_accessed=2 * hidden.shape[1] * inner + 4 * length * inner,
            transcendentals=0,
        ),
        name="project",
    )(hidden, weight)


def mixer_forward(keep, bound, x, x_proj, dt_proj, params, decay2, *, tokens, inner, states, rank, taps, slots):
    blocks, tiles, octets = inner // 1024, inner // 128, tokens // 8
    size = octets // slots
    rows = tokens * tiles

    def body(keep_ref, bound_ref, x_ref, xw_ref, dt_ref, p_ref, a_ref, y_ref, sf_ref, sr_ref, df_ref, dr_ref, proj_ref, bc_ref):
        shape4 = (octets, tiles, 8, 128)
        y4 = y_ref.reshape(shape4)
        s4 = (sf_ref.reshape(shape4), sr_ref.reshape(shape4))
        d4 = (df_ref.reshape(shape4), dr_ref.reshape(shape4))

        def conv(k, _):
            p = p_ref[k]
            skip = p[taps + 2 : taps + 3][None]
            for q in range(slots):
                both, _ = convolved(extended(x_ref, k, q, size, bound_ref, slots), p, taps)
                sl = pl.ds(q * size, size)
                series = [c * jax.nn.sigmoid(c) for c in both]
                for ref, v in zip(s4, series):
                    ref[sl, k] = v
                y4[sl, k] = skip * (series[0] + series[1])
            return 0

        lax.fori_loop(0, tiles, conv, 0)
        lanes = lax.broadcasted_iota(jnp.int32, (tokens, 128), 1)
        for s in range(2):
            total = jnp.zeros((tokens, 128), F32)
            for k in range(0, tiles, 2):
                lhs = jnp.concatenate(
                    [s4[s][:, k + i].reshape(tokens, 128).astype(BF16) for i in range(2)], axis=1
                )
                total = total + dot(lhs, xw_ref[pl.ds(k * 128, 256), :])
            proj_ref[s] = total
            low = jnp.where(lanes < rank, total, 0.0).astype(BF16)
            for k in range(0, tiles, 2):
                pre = dot_nt(low, dt_ref[pl.ds(k * 128, 256), :])
                for i in range(2):
                    v = pre[:, i * 128 : (i + 1) * 128] + p_ref[k + i, taps + 1 : taps + 2, :]
                    step = jnp.maximum(v, 0.0) + jnp.log1p(jnp.exp(-jnp.abs(v)))
                    d4[s][:, k + i] = step.reshape(octets, 8, 128)
        for s, (d_ref, u_ref) in enumerate(((df_ref, sf_ref), (dr_ref, sr_ref))):
            rev = s == 1
            for ng in range(states // GROUP):
                fill_columns(proj_ref.at[s], bc_ref, tokens, rank, ng, states)
                a = [
                    [a_ref[pl.ds((ng * GROUP + n) * tiles + c * 8, 8), :] for c in range(blocks)]
                    for n in range(GROUP)
                ]

                def octet(i, hs):
                    g = (octets - 1 - i) if rev else i
                    keep_now = keep_ref[s, i]
                    hs = [h * keep_now for h in hs]
                    base = pl.multiple_of(g * (tiles * 8), 8)
                    for j in range(8):
                        tt = 7 - j if rev else j
                        t = g * 8 + tt
                        for c in range(blocks):
                            sl = pl.ds(base + c * 64 + tt, 8, stride=8)
                            d = d_ref[sl, :]
                            du = d * u_ref[sl, :]
                            acc = None
                            for n in range(GROUP):
                                b = bc_ref[pl.ds(n * tokens + t, 1), :]
                                cc = bc_ref[pl.ds((GROUP + n) * tokens + t, 1), :]
                                k = n * blocks + c
                                hs[k] = jnp.exp2(d * a[n][c]) * hs[k] + du * b
                                acc = hs[k] * cc if acc is None else acc + hs[k] * cc
                            y_ref[sl, :] = y_ref[sl, :] + acc
                    return hs

                lax.fori_loop(0, octets, octet, [jnp.zeros((8, 128), F32)] * (GROUP * blocks))

    big = jax.ShapeDtypeStruct((rows, 128), F32)
    return pl.pallas_call(
        body,
        out_shape=(big,) * 5 + (jax.ShapeDtypeStruct((2, tokens, 128), F32),),
        in_specs=[SMEM, SMEM] + [VMEM] * 5,
        out_specs=(VMEM,) * 6,
        scratch_shapes=[pltpu.VMEM((2 * GROUP * tokens, 128), F32)],
        compiler_params=pltpu.CompilerParams(vmem_limit_bytes=56 << 20),
        cost_estimate=pl.CostEstimate(
            flops=tokens * inner * states * 160,
            bytes_accessed=6 * rows * 512,
            transcendentals=2 * tokens * inner * states,
        ),
        name="mixer_forward",
    )(keep, bound, x, x_proj, dt_proj, params, decay2)


def mixer_middle(place, hidden, weight, out_weight, branch_grad, total, *, rows, length, inner):
    blocks, owners, _, cols = weight.shape[0], weight.shape[1], 0, weight.shape[-1]
    packed = out_weight is None
    dp, per, wide = branch_grad.shape[0], owners // blocks, branch_grad.shape[2]
    tiles, octets = cols // 128, length // 8
    half = rows
    width = hidden.shape[1]

    def body(place_ref, h_ref, wz_ref, wo_ref, bg_ref, t_ref, g_ref, dz_ref, br_ref, *more):
        ml_ref, gz_ref, go_ref, ht_ref, sem = more[-5:]
        b = pl.program_id(0)
        where = place_ref[b]

        def copies():
            if packed:
                return [
                    pltpu.make_async_copy(gz_ref, more[0].at[b, :, 0], sem.at[0]),
                    pltpu.make_async_copy(go_ref, more[0].at[:, pl.ds(where * per, per), 1], sem.at[1]),
                ]
            return [
                pltpu.make_async_copy(gz_ref, more[0].at[b], sem.at[0]),
                pltpu.make_async_copy(go_ref, more[1].at[:, pl.ds(where * per, per)], sem.at[1]),
            ]

        z = dot(h_ref[...], wz_ref[...].reshape(owners * rows, cols))

        def out_rows(d):
            if not packed:
                return wo_ref[d].reshape(cols, wide)
            pieces = []
            for j in range(per):
                for i in range(2):
                    pieces.append(wo_ref[d, j, 0, :, i * wide : (i + 1) * wide])
            return jnp.concatenate(pieces, axis=0)

        mg = dot_nt(bg_ref[0], out_rows(0))
        for d in range(1, dp):
            mg = mg + dot_nt(bg_ref[d], out_rows(d))
        for k in range(tiles):
            sl = slice(k * 128, (k + 1) * 128)
            zk, mk, tk = z[:, sl], mg[:, sl], t_ref[:, k].reshape(length, 128)
            gate = jax.nn.sigmoid(zk)
            silu = zk * gate
            ml_ref[:, sl] = (tk * silu).astype(BF16)
            g_ref[:, k] = (mk * silu).reshape(octets, 8, 128)
            dz_ref[:, sl] = (mk * tk * (gate * (1.0 + zk * (1.0 - gate)))).astype(BF16)
        ml = ml_ref[...]
        ml_t = ml.T

        @pl.when(b == 0)
        def _():
            br_ref[...] = jnp.zeros_like(br_ref)
            ht_ref[...] = h_ref[...].T

        @pl.when(b > 0)
        def _():
            for c in copies():
                c.wait()

        for d in range(dp):
            br_ref[d] = br_ref[d] + dot(ml, out_rows(d))
            go = dot(ml_t, bg_ref[d]).astype(BF16)
            if packed:
                at = 0
                for j in range(per):
                    for i in range(2):
                        go_ref[d, j, :, i * wide : (i + 1) * wide] = go[at : at + half]
                        at += half
            else:
                go_ref[d] = go.reshape(go_ref.shape[1:])
        gz_ref[...] = dot(ht_ref[...], dz_ref[...]).astype(BF16).reshape(owners, rows, cols)
        for c in copies():
            c.start()

        @pl.when(b == blocks - 1)
        def _():
            for c in copies():
                c.wait()

    if packed:
        wz_spec = pl.BlockSpec((1, owners, 1, rows, cols), lambda b, p: (b, 0, 0, 0, 0))
        wo_spec = pl.BlockSpec((dp, per, 1, rows, cols), lambda b, p: (0, p[b], 1, 0, 0))
        extra = (jax.ShapeDtypeStruct((blocks, owners, 2, rows, cols), BF16),)
        go_shape = (dp, per, rows, cols)
        out_weight = weight
    else:
        wz_spec = pl.BlockSpec((1, owners, rows, cols), lambda b, p: (b, 0, 0, 0))
        wo_spec = pl.BlockSpec((dp, per, 2 * rows, wide), lambda b, p: (0, p[b], 0, 0))
        extra = (
            jax.ShapeDtypeStruct((blocks, owners, rows, cols), BF16),
            jax.ShapeDtypeStruct((dp, owners, 2 * rows, wide), BF16),
        )
        go_shape = (dp, per, 2 * rows, wide)
    whole = lambda v: pl.BlockSpec(v.shape, lambda b, p: (0,) * v.ndim)
    tile_spec = pl.BlockSpec((octets, tiles, 8, 128), lambda b, p: (0, b, 0, 0))
    return pl.pallas_call(
        body,
        grid_spec=pltpu.PrefetchScalarGridSpec(
            num_scalar_prefetch=1,
            grid=(blocks,),
            in_specs=[
                whole(hidden),
                wz_spec,
                wo_spec,
                whole(branch_grad),
                tile_spec,
            ],
            out_specs=(
                tile_spec,
                pl.BlockSpec((length, cols), lambda b, p: (0, b)),
                pl.BlockSpec((dp, length, wide), lambda b, p: (0, 0, 0)),
            )
            + (ANY,) * len(extra),
            scratch_shapes=[
                pltpu.VMEM((length, cols), BF16),
                pltpu.VMEM((owners, rows, cols), BF16),
                pltpu.VMEM(go_shape, BF16),
                pltpu.VMEM((width, length), BF16),
                pltpu.SemaphoreType.DMA((2,)),
            ],
        ),
        out_shape=(
            jax.ShapeDtypeStruct((octets, inner // 128, 8, 128), F32),
            jax.ShapeDtypeStruct((length, inner), BF16),
            jax.ShapeDtypeStruct((dp, length, wide), F32),
        )
        + extra,
        compiler_params=pltpu.CompilerParams(vmem_limit_bytes=56 << 20),
        cost_estimate=pl.CostEstimate(
            flops=10 * length * width * inner, bytes_accessed=60 << 20, transcendentals=length * inner
        ),
        name="mixer_middle",
    )(place, hidden, weight, out_weight, branch_grad, total)


def mixer_backward(keep, proj, step, series, grad, decay2, x_proj, dt_proj, params, *, rev, tokens, inner, states, rank, taps):
    blocks, tiles, octets = inner // 1024, inner // 128, tokens // 8
    slots = GROUP * blocks
    rows = tokens * tiles

    def body(
        keep_ref, proj_ref, d_ref, u_ref, g_ref, a_ref, xw_ref, dt_ref, p_ref,
        ddu_ref, small_ref, da_ref, skip_ref,
        dd_ref, bc_ref, h_ref, q_ref, r_ref, cols_ref,
    ):
        zero = jnp.zeros((8, 128), F32)
        cols_ref[...] = jnp.zeros_like(cols_ref)
        for ng in range(states // GROUP):
            fill_columns(proj_ref, bc_ref, tokens, rank, ng, states)
            a = [
                [a_ref[pl.ds((ng * GROUP + n) * tiles + c * 8, 8), :] for c in range(blocks)]
                for n in range(GROUP)
            ]
            for k in range(slots):
                h_ref[pl.ds(k * 8, 8), :] = zero

            def ahead(i, hs):
                g = (octets - 1 - i) if rev else i
                keep_now = keep_ref[i]
                hs = [h * keep_now for h in hs]
                base = pl.multiple_of(g * (tiles * 8), 8)
                for j in range(8):
                    tt = 7 - j if rev else j
                    t = g * 8 + tt
                    hb = pl.multiple_of((i * 8 + j + 1) * (slots * 8), 8)
                    for c in range(blocks):
                        sl = pl.ds(base + c * 64 + tt, 8, stride=8)
                        d = d_ref[sl, :]
                        du = d * u_ref[sl, :]
                        for n in range(GROUP):
                            b = bc_ref[pl.ds(n * tokens + t, 1), :]
                            k = n * blocks + c
                            hs[k] = jnp.exp2(d * a[n][c]) * hs[k] + du * b
                            h_ref[pl.ds(hb + k * 8, 8), :] = hs[k]
                return hs

            lax.fori_loop(0, octets, ahead, [zero] * slots)

            def back(ii, carry):
                gs, das = [list(v) for v in carry]
                i = octets - 1 - ii
                g = (octets - 1 - i) if rev else i
                keep_now = keep_ref[i]
                base = pl.multiple_of(g * (tiles * 8), 8)
                for jj in range(8):
                    j = 7 - jj
                    tt = 7 - j if rev else j
                    t = g * 8 + tt
                    hb = pl.multiple_of((i * 8 + j) * (slots * 8), 8)
                    pb, pc = [None] * GROUP, [None] * GROUP
                    for c in range(blocks):
                        sl = pl.ds(base + c * 64 + tt, 8, stride=8)
                        d = d_ref[sl, :]
                        du = d * u_ref[sl, :]
                        gy = g_ref[sl, :]
                        ddu = dd = None
                        for n in range(GROUP):
                            b = bc_ref[pl.ds(n * tokens + t, 1), :]
                            cc = bc_ref[pl.ds((GROUP + n) * tokens + t, 1), :]
                            k = n * blocks + c
                            before = h_ref[pl.ds(hb + k * 8, 8), :]
                            after = h_ref[pl.ds(hb + (slots + k) * 8, 8), :]
                            adj = gs[k] + cc * gy
                            x = after * gy
                            pc[n] = x if c == 0 else pc[n] + x
                            x = adj * du
                            pb[n] = x if c == 0 else pb[n] + x
                            x = adj * b
                            ddu = x if n == 0 else ddu + x
                            moved = adj * jnp.exp2(d * a[n][c])
                            if j == 0:
                                moved = moved * keep_now
                            gs[k] = moved
                            m = moved * before
                            x = m * a[n][c]
                            dd = x if n == 0 else dd + x
                            das[k] = das[k] + m * d
                        if ng == 0:
                            ddu_ref[sl, :] = ddu
                            dd_ref[sl, :] = dd
                        else:
                            ddu_ref[sl, :] = ddu_ref[sl, :] + ddu
                            dd_ref[sl, :] = dd_ref[sl, :] + dd
                    for n in range(GROUP):
                        q_ref[pl.ds(j * 64 + n * 8, 8), :] = pb[n]
                        q_ref[pl.ds(j * 64 + (GROUP + n) * 8, 8), :] = pc[n]
                for j in range(8):
                    tt = 7 - j if rev else j
                    t = g * 8 + tt
                    s = None
                    for q in range(8):
                        x = q_ref[pl.ds(j * 64 + q, 8, stride=8), :]
                        s = x if s is None else s + x
                    r_ref[pl.ds(pl.multiple_of(t * 8, 8), 8), :] = s
                return gs, das

            _, das = lax.fori_loop(0, octets, back, ([zero] * slots, [zero] * slots))
            for n in range(GROUP):
                for c in range(blocks):
                    da_ref[pl.ds((ng * GROUP + n) * tiles + c * 8, 8), :] = das[n * blocks + c]
            lane = lax.broadcasted_iota(jnp.int32, (128, 128), 1)
            for q in range(2 * GROUP):
                col = rank + (q // GROUP) * states + ng * GROUP + q % GROUP
                one = jnp.where(lane == col, 1.0, 0.0).astype(BF16)
                v = r_ref[pl.ds(q, tokens, stride=8), :]
                high_part = v.astype(BF16)
                low_part = (v - high_part.astype(F32)).astype(BF16)
                cols_ref[...] += dot(high_part, one) + dot(low_part, one)
        shape4 = (octets, tiles, 8, 128)
        d4, u4, g4, ddu4, dd4 = [r.reshape(shape4) for r in (d_ref, u_ref, g_ref, ddu_ref, dd_ref)]
        lanes = lax.broadcasted_iota(jnp.int32, (tokens, 128), 1)
        low = jnp.where(lanes < rank, proj_ref[...], jnp.where(lanes == rank, 1.0, 0.0)).astype(BF16)
        low_t = low.T
        proj_grad = jnp.zeros((tokens, 128), F32)
        for k in range(0, tiles, 2):
            pair = []
            for i in range(2):
                d, u, gy, ddu = d4[:, k + i], u4[:, k + i], g4[:, k + i], ddu4[:, k + i]
                pre = (ddu * u + LN2 * dd4[:, k + i]) * (1.0 - jnp.exp(-d))
                pair.append(pre.reshape(tokens, 128).astype(BF16))
                ddu4[:, k + i] = ddu * d + p_ref[k + i, taps + 2 : taps + 3, :][None] * gy
                skip_ref[k + i] = jnp.sum(gy * u, axis=0)
            pre = jnp.concatenate(pair, axis=1)
            proj_grad = proj_grad + dot(pre, dt_ref[pl.ds(k * 128, 256), :])
            small_ref[128:256, k * 128 : (k + 2) * 128] = dot(low_t, pre)
        proj_grad = jnp.where(lanes < rank, proj_grad, cols_ref[...]).astype(BF16)
        proj_t = proj_grad.T
        for k in range(0, tiles, 2):
            pair = [u4[:, k + i].reshape(tokens, 128).astype(BF16) for i in range(2)]
            small_ref[0:128, k * 128 : (k + 2) * 128] = dot(proj_t, jnp.concatenate(pair, axis=1))
            more = dot_nt(proj_grad, xw_ref[pl.ds(k * 128, 256), :])
            for i in range(2):
                ddu4[:, k + i] = ddu4[:, k + i] + more[:, i * 128 : (i + 1) * 128].reshape(octets, 8, 128)

    return pl.pallas_call(
        body,
        out_shape=(
            jax.ShapeDtypeStruct((rows, 128), F32),
            jax.ShapeDtypeStruct((256, inner), F32),
            jax.ShapeDtypeStruct((states * tiles, 128), F32),
            jax.ShapeDtypeStruct((tiles, 8, 128), F32),
        ),
        in_specs=[SMEM] + [VMEM] * 8,
        out_specs=(VMEM,) * 4,
        scratch_shapes=[
            pltpu.VMEM((rows, 128), F32),
            pltpu.VMEM((2 * GROUP * tokens, 128), F32),
            pltpu.VMEM((slots * 8 * (tokens + 1), 128), F32),
            pltpu.VMEM((512, 128), F32),
            pltpu.VMEM((tokens * 8, 128), F32),
            pltpu.VMEM((tokens, 128), F32),
        ],
        compiler_params=pltpu.CompilerParams(vmem_limit_bytes=60 << 20),
        cost_estimate=pl.CostEstimate(
            flops=tokens * inner * states * 160,
            bytes_accessed=5 * rows * 512,
            transcendentals=2 * tokens * inner * states,
        ),
        name="mixer_backward",
    )(keep, proj, step, series, grad, decay2, x_proj, dt_proj, params)


def mixer_finish(bound, x, grads, params, hidden, z_grad, wx, wz, *, rows, total_rows, length, inner, taps, slots):
    blocks, owners, cols = wx.shape[0], wx.shape[1], wx.shape[-1]
    tiles, octets = cols // 128, length // 8
    size = octets // slots
    width = hidden.shape[1]
    packed = wz.ndim == 5

    def body(bound_ref, x_ref, gf_ref, gr_ref, p_ref, h_ref, dz_ref, wx_ref, wz_ref, gx_ref, hg_ref, gw_ref, cf_ref, cr_ref, dx_ref, ht_ref):
        def first(k, _):
            p = p_ref[k]
            sums = [jnp.zeros((8, 128), F32) for _ in range(taps + 1)]
            for q in range(slots):
                ext = extended(x_ref, k, q, size, bound_ref, slots)
                both, moves = convolved(ext, p, taps)
                sl = pl.ds(q * size, size)
                for s, (c, src, dst) in enumerate(zip(both, (gf_ref, gr_ref), (cf_ref, cr_ref))):
                    gate = jax.nn.sigmoid(c)
                    dc = src[sl, k] * (gate * (1.0 + c * (1.0 - gate)))
                    dst[sl, k] = dc
                    sums[taps] = sums[taps] + jnp.sum(dc, axis=0)
                    sums[taps - 1] = sums[taps - 1] + jnp.sum(dc * ext[1:-1], axis=0)
                    for j in range(1, taps):
                        m = moves[s * (taps - 1) + j - 1]
                        sums[taps - 1 - j] = sums[taps - 1 - j] + jnp.sum(dc * m, axis=0)
            for i, v in enumerate(sums):
                gw_ref[k, i] = v
            return 0

        @pl.when(pl.program_id(0) == 0)
        def _():
            ht_ref[...] = h_ref[...].T

        lax.fori_loop(0, tiles, first, 0)
        for k in range(tiles):
            p = p_ref[k]
            for q in range(slots):
                ef = extended(cf_ref, k, q, size, bound_ref, slots)
                er = extended(cr_ref, k, q, size, bound_ref, slots)
                v = p[taps - 1 : taps][None] * (ef[1:-1] + er[1:-1])
                for j in range(1, taps):
                    v = v + p[taps - 1 - j : taps - j][None] * (shifted(ef, j, True) + shifted(er, j, False))
                dx_ref[pl.ds(q * size * 8, size * 8), k * 128 : (k + 1) * 128] = v.reshape(size * 8, 128).astype(BF16)
        dx = dx_ref[...]
        gx_ref[0] = dot(ht_ref[...], dx).astype(BF16).reshape(owners, rows, cols)
        hg = dot_nt(dx, wx_ref[...].reshape(owners * rows, cols)) + dot_nt(
            dz_ref[...], wz_ref[...].reshape(owners * rows, cols)
        )

        @pl.when(pl.program_id(0) == 0)
        def _():
            hg_ref[...] = hg

        @pl.when(pl.program_id(0) > 0)
        def _():
            hg_ref[...] = hg_ref[...] + hg

    tile_spec = pl.BlockSpec((octets, tiles, 8, 128), lambda b: (0, b, 0, 0))
    w_spec = pl.BlockSpec((1, owners, rows, cols), lambda b: (b, 0, 0, 0))
    z_spec = pl.BlockSpec((1, owners, 1, rows, cols), lambda b: (b, 0, 0, 0, 0)) if packed else w_spec
    return pl.pallas_call(
        body,
        grid=(blocks,),
        in_specs=[
            SMEM,
            tile_spec,
            tile_spec,
            tile_spec,
            pl.BlockSpec((tiles, 8, 128), lambda b: (b, 0, 0)),
            pl.BlockSpec(hidden.shape, lambda b: (0, 0)),
            pl.BlockSpec((length, cols), lambda b: (0, b)),
            w_spec,
            z_spec,
        ],
        out_specs=(
            pl.BlockSpec((1, owners, rows, cols), lambda b: (b, 0, 0, 0)),
            pl.BlockSpec((length, width), lambda b: (0, 0)),
            pl.BlockSpec((tiles, taps + 1, 8, 128), lambda b: (b, 0, 0, 0)),
        ),
        out_shape=(
            jax.ShapeDtypeStruct((blocks, owners, total_rows, cols), BF16),
            jax.ShapeDtypeStruct((length, width), F32),
            jax.ShapeDtypeStruct((inner // 128, taps + 1, 8, 128), F32),
        ),
        scratch_shapes=[
            pltpu.VMEM((octets, tiles, 8, 128), F32),
            pltpu.VMEM((octets, tiles, 8, 128), F32),
            pltpu.VMEM((length, cols), BF16),
            pltpu.VMEM((width, length), BF16),
        ],
        compiler_params=pltpu.CompilerParams(vmem_limit_bytes=56 << 20),
        cost_estimate=pl.CostEstimate(
            flops=6 * length * width * inner, bytes_accessed=45 << 20, transcendentals=2 * length * inner
        ),
        name="mixer_finish",
    )(bound, x, grads[0], grads[1], params, hidden, z_grad, wx, wz)


def swap(v, axis, k):
    return lax.ppermute(v, axis, [(i, i ^ k) for i in range(lax.axis_size(axis))])


def others(v, axis):
    return jnp.stack([v] + [swap(v, axis, k) for k in range(1, lax.axis_size(axis))])


def gather_all(v):
    return others(others(others(v, "dp"), "fz"), "core")


def per_device(
    tokens,
    segment,
    timestep,
    ada_weight,
    ada_bias,
    in_weight,
    conv_weight,
    convolution_bias,
    xproj_weight,
    dtproj_weight,
    dt_bias,
    a_log,
    d_skip,
    out_weight,
    cotangent,
):
    dp, fz, cores = [lax.axis_size(n) for n in ALL]
    my_dp = lax.axis_index("dp")
    my_j = lax.axis_index("fz") * cores + lax.axis_index("core")
    fsdp = fz * cores
    devices = dp * fsdp
    slots = timestep.shape[0]
    length, width = tokens.shape
    taps, rank, states = conv_weight.shape[1], dtproj_weight.shape[1], a_log.shape[1]
    own = conv_weight.shape[0]
    inner = own * devices
    rows, cols = in_weight.shape[0], in_weight.shape[1] // 2
    wide = out_weight.shape[1]
    packs = wide % 128 == 0
    contract_rows = (((0,), (0,)), ((), ()))

    lower = my_dp < dp // 2
    opposite = [(i, (i + dp // 2) % dp) for i in range(dp)]
    left, right = in_weight[:, :cols], in_weight[:, cols:]
    got = lax.ppermute(jnp.where(lower, right, left), "dp", opposite)
    kept = jnp.where(lower, left, right)
    x_cols, z_cols = jnp.where(lower, kept, got), jnp.where(lower, got, kept)
    order = [(b % (dp // 2)) * 2 + b // (dp // 2) for b in range(dp)]

    parts = [
        xproj_weight,
        dtproj_weight,
        conv_weight,
        convolution_bias[:, None],
        dt_bias[:, None],
        d_skip[:, None],
        a_log,
    ]
    packed = jnp.concatenate(parts, axis=1)
    packed = jnp.pad(packed, ((0, 0), (0, 256 - packed.shape[1])))
    tail = own * 256 // cols
    g_x = lax.all_gather(jnp.concatenate([x_cols, packed.reshape(tail, cols)], axis=0), ALL, axis=0, tiled=True)
    g_x = g_x.reshape(dp, fsdp, rows + tail, cols)
    times = gather_all(timestep).reshape(-1)
    ada_rows, ada_cols = ada_weight.shape
    condition = embed_columns(
        times, my_j * ada_rows + jnp.arange(ada_rows, dtype=jnp.int32), width
    ).astype(BF16)
    bias_cols = ada_bias.shape[0]
    bias_part = lax.dynamic_update_slice(
        jnp.zeros((ada_cols,), F32), ada_bias.astype(F32), (my_j * bias_cols,)
    )
    partial = jnp.dot(condition, ada_weight, preferred_element_type=F32) + bias_part[None, :]
    partial = partial.reshape(cores, fz, dp, slots, ada_cols)
    for axis, n in (("core", cores), ("fz", fz)):
        partial = partial[0] + sum(swap(partial[k], axis, k) for k in range(1, n))
    blocks = jnp.stack([partial[0]] + [swap(partial[k], "dp", k) for k in range(1, dp)])
    modulation = jnp.concatenate(
        [lax.dynamic_index_in_dim(blocks, my_dp ^ b, keepdims=False) for b in range(dp)], axis=1
    )
    picker = (segment[:, None] == jnp.arange(slots, dtype=jnp.int32)[None, :]).astype(F32)
    per_token = jnp.dot(picker, modulation, precision=high)
    shift_mod = per_token[:, :width]
    scale_mod = per_token[:, width : 2 * width]
    gate_mod = per_token[:, 2 * width :]
    centered = tokens - jnp.mean(tokens, axis=1, keepdims=True)
    inv_std = lax.rsqrt(jnp.mean(centered * centered, axis=1, keepdims=True) + 1e-06)
    normed = centered * inv_std
    hidden = (normed * (1.0 + scale_mod) + shift_mod).astype(BF16)
    branch_grad = (cotangent * gate_mod).astype(BF16)
    branch_grad = branch_grad.reshape(length, dp, wide).transpose(1, 0, 2)

    if packs:
        out_piece = jnp.concatenate([out_weight[:rows], out_weight[rows:]], axis=1)
        later = jnp.stack([z_cols, out_piece])
        later, g_x, hidden = lax.optimization_barrier((later, g_x, hidden))
        g_z = lax.all_gather(later, ALL, axis=0, tiled=True).reshape(dp, fsdp, 2, rows, cols)
        g_out = None
    else:
        g_z = lax.all_gather(z_cols, ALL, axis=0, tiled=True).reshape(dp, fsdp, rows, cols)
        g_out = lax.all_gather(out_weight, ALL, axis=0, tiled=True).reshape(dp, fsdp, 2 * rows, wide)

    packed = g_x[:, :, rows:, :].reshape(dp, inner // dp, 256)
    packed = jnp.concatenate([packed[o] for o in order], axis=0)
    x_proj, dt_proj = packed[:, :128], packed[:, 128:256]
    rest = packed[:, 128 + rank :].astype(F32).T
    params = rest[:8].reshape(8, inner // 128, 128).transpose(1, 0, 2)
    decay = -jnp.exp(rest[taps + 3 : taps + 3 + states])
    decay2 = (decay * (1.0 / LN2)).reshape(states * inner // 128, 128)

    same = (segment[1:] == segment[:-1]).astype(F32)
    same = jnp.concatenate([jnp.zeros((1,), F32), same, jnp.zeros((1,), F32)])
    keep_f, keep_r = same[0:length:8], same[8 : length + 1 : 8][::-1]
    bound = same[0 : length : length // slots]
    sizes = dict(tokens=length, inner=inner, states=states, rank=rank, taps=taps)

    x = project(hidden, g_x, rows=rows, length=length, inner=inner)
    total, series_f, series_r, step_f, step_r, proj = mixer_forward(
        jnp.stack([keep_f, keep_r]), bound, x, x_proj, dt_proj, params, decay2, slots=slots, **sizes
    )
    tile_shape = (length // 8, inner // 128, 8, 128)
    middle = mixer_middle(
        jnp.asarray(order, jnp.int32),
        hidden,
        g_z,
        g_out,
        branch_grad,
        total.reshape(tile_shape),
        rows=rows,
        length=length,
        inner=inner,
    )
    grad, z_grad, branch = middle[:3]
    branch = branch.transpose(1, 0, 2).reshape(length, width)
    layer_out = tokens + gate_mod * branch
    gate_grad = cotangent * branch

    def scattered(v):
        return lax.psum_scatter(v.reshape(-1, v.shape[-1]), ALL, scatter_dimension=0, tiled=True)

    if packs:
        early = scattered(middle[3])
        z_shard, out_shard = early[:rows], early[rows:]
        out_shard = jnp.concatenate([out_shard[:, :wide], out_shard[:, wide:]], axis=0)
    else:
        z_shard, out_shard = early = scattered(middle[3]), scattered(middle[4])

    grad = grad.reshape(total.shape)
    series_grad, small, da, skip_part = [], 0.0, 0.0, 0.0
    for k, (keep, step, series) in enumerate(((keep_f, step_f, series_f), (keep_r, step_r, series_r))):
        got = mixer_backward(
            keep, proj[k], step, series, grad, decay2, x_proj, dt_proj, params, rev=k == 1, **sizes
        )
        series_grad.append(got[0].reshape(tile_shape))
        small, da, skip_part = small + got[1], da + got[2], skip_part + got[3]

    g_in, hidden_grad, conv_part = mixer_finish(
        bound,
        x,
        series_grad,
        params,
        hidden,
        z_grad,
        g_x,
        g_z,
        rows=rows,
        total_rows=rows + tail,
        length=length,
        inner=inner,
        taps=taps,
        slots=slots,
    )
    conv_rows = conv_part.sum(axis=2).transpose(1, 0, 2).reshape(taps + 1, inner)
    small_t = jnp.concatenate(
        [
            small[: 128 + rank],
            conv_rows,
            small[128 + rank : 128 + rank + 1],
            skip_part.sum(axis=1).reshape(1, inner),
            da.reshape(states, inner) * decay,
            jnp.zeros((256 - 128 - rank - taps - 3 - states, inner), F32),
        ],
        axis=0,
    ).astype(BF16)
    small = small_t.T.reshape(dp, inner // dp, 256)
    small = jnp.concatenate([small[order.index(o)] for o in range(dp)], axis=0)
    g_in = lax.dynamic_update_slice(g_in, small.reshape(dp, fsdp, tail, cols), (0, 0, rows, 0))
    g_in, _ = lax.optimization_barrier((g_in, early))
    got = scattered(g_in)
    x_shard, small = got[:rows], got[rows:].reshape(own, 256).astype(F32)
    got = lax.ppermute(jnp.where(lower, z_shard, x_shard), "dp", opposite)
    grad_in_shard = jnp.where(
        lower,
        jnp.concatenate([x_shard, got], axis=1),
        jnp.concatenate([got, z_shard], axis=1),
    ).astype(F32)

    normed_grad = hidden_grad * (1.0 + scale_mod)
    grad_tokens = cotangent + inv_std * (
        normed_grad
        - jnp.mean(normed_grad, axis=1, keepdims=True)
        - normed * jnp.mean(normed_grad * normed, axis=1, keepdims=True)
    )
    token_mod_grad = jnp.concatenate([hidden_grad, hidden_grad * normed, gate_grad], axis=1)
    mod_low = lax.dot_general(picker, token_mod_grad, contract_rows, precision=high).astype(BF16)
    mod_all = gather_all(mod_low).reshape(devices * slots, dp * ada_cols)
    mod_cols = lax.dynamic_slice_in_dim(mod_all, my_dp * ada_cols, ada_cols, axis=1)
    grad_ada_w = lax.dot_general(condition, mod_cols, contract_rows, preferred_element_type=F32)
    grad_ada_b = jnp.sum(
        lax.dynamic_slice_in_dim(mod_cols, my_j * bias_cols, bias_cols, axis=1).astype(F32), axis=0
    )
    valid = (segment < slots).astype(F32)[:, None]
    sums = jnp.stack(
        [
            jnp.sum(layer_out * layer_out * valid),
            jnp.sum(grad_tokens * grad_tokens * valid),
            jnp.sum(valid) * width,
        ]
    )
    sums = jnp.sum(gather_all(jnp.pad(sums, (0, 125))).reshape(devices, 128), axis=0)
    out_sq, grad_sq, counted = sums[0], sums[1], sums[2]
    at = 128 + rank
    return (
        layer_out,
        grad_tokens,
        grad_ada_w,
        grad_ada_b,
        grad_in_shard,
        small[:, at : at + taps],
        small[:, at + taps],
        small[:, :128],
        small[:, 128:at],
        small[:, at + taps + 1],
        small[:, at + taps + 3 : at + taps + 3 + states],
        small[:, at + taps + 2],
        out_shard.astype(F32),
        jnp.sqrt(out_sq / counted),
        jnp.sqrt(grad_sq / counted),
    )


def solution(mesh):
    dp, fsdp = mesh.devices.shape
    cores = 2 if fsdp % 2 == 0 else 1
    split = Mesh(mesh.devices.reshape(dp, fsdp // cores, cores), ALL)
    rows, flat, block = P(ALL, None), P(ALL), P(("fz", "core"), "dp")
    return jax.shard_map(
        per_device,
        mesh=split,
        in_specs=(
            rows, flat, flat, block, flat, block, rows, flat, rows, rows, flat, rows, flat, block, rows,
        ),
        out_specs=(
            rows, rows, block, flat, block, rows, flat, rows, rows, flat, rows, flat, block, P(), P(),
        ),
        check_vma=False,
    )
```

```python
import math

import jax
import jax.numpy as jnp
from jax import lax
from jax.experimental import pallas as pl
from jax.experimental.pallas import tpu as pltpu
from jax.sharding import Mesh, PartitionSpec as P

F32 = jnp.float32
BF16 = jnp.bfloat16
LN2 = math.log(2.0)
ALL = ("dp", "fz", "core")
high = lax.Precision.HIGHEST
GROUP = 4


def embed_columns(time_values, column, model_width):
    half_width = model_width // 2
    lower_half = column < half_width
    freq_index = jnp.where(lower_half, column, column - half_width).astype(F32)
    frequency = jnp.exp(freq_index * (-math.log(10000.0) / half_width))
    angles = time_values.astype(F32)[:, None] * frequency[None, :]
    return jax.nn.silu(jnp.where(lower_half[None, :], jnp.cos(angles), jnp.sin(angles)))


def fill_columns(proj_ref, bc_ref, tokens, first, group, states):
    def fill(i, _):
        p = proj_ref[pl.ds(pl.multiple_of(i * 8, 8), 8), :]
        for s in range(2):
            for n in range(GROUP):
                col = first + s * states + group * GROUP + n
                row = pl.multiple_of((s * GROUP + n) * tokens + i * 8, 8)
                bc_ref[pl.ds(row, 8), :] = jnp.broadcast_to(p[:, col : col + 1], (8, 128))
        return 0

    lax.fori_loop(0, tokens // 8, fill, 0, unroll=8)


VMEM = pl.BlockSpec(memory_space=pltpu.VMEM)
SMEM = pl.BlockSpec(memory_space=pltpu.SMEM)
ANY = pl.BlockSpec(memory_space=pl.ANY)


def dot(a, b):
    return jnp.dot(a, b, preferred_element_type=F32)


def dot_nt(a, b):
    return lax.dot_general(a, b, (((1,), (1,)), ((), ())), preferred_element_type=F32)


def shifted(ext, j, ahead):
    n = ext.shape[0] - 2
    sub = lax.broadcasted_iota(jnp.int32, (n, 8, 128), 1)
    if ahead:
        r = pltpu.roll(ext, 8 - j, 1)
        return jnp.where(sub >= 8 - j, r[2:], r[1:-1])
    r = pltpu.roll(ext, j, 1)
    return jnp.where(sub < j, r[:-2], r[1:-1])


def extended(ref, k, q, size, keep_ref, slots):
    zero = jnp.zeros((1, 8, 128), F32)
    lo, hi = q * size, (q + 1) * size
    before = ref[pl.ds(lo - 1, 1), k] * keep_ref[q] if q else zero
    after = ref[pl.ds(hi, 1), k] * keep_ref[q + 1] if q < slots - 1 else zero
    return jnp.concatenate([before, ref[pl.ds(lo, size), k], after], axis=0)


def convolved(ext, p, taps):
    here = ext[1:-1]
    both, moves = [], []
    for ahead in (False, True):
        c = p[taps : taps + 1][None] + p[taps - 1 : taps][None] * here
        for j in range(1, taps):
            m = shifted(ext, j, ahead)
            moves.append(m)
            c = c + p[taps - 1 - j : taps - j][None] * m
        both.append(c)
    return both, moves


def sublane_sums(vs):
    sub = lax.broadcasted_iota(jnp.int32, (8, 128), 0)
    for sh in (4, 2, 1):
        upper = (sub & sh) != 0
        half = len(vs) // 2
        vs = [
            jnp.where(
                upper,
                vs[q + half] + pltpu.roll(vs[q + half], sh, 0),
                vs[q] + pltpu.roll(vs[q], 8 - sh, 0),
            )
            for q in range(half)
        ]
    return vs[0]


def project(hidden, weight, *, rows, length, inner):
    blocks, owners, _, cols = weight.shape
    tiles = cols // 128

    def body(h_ref, w_ref, o_ref):
        w = w_ref[0].reshape(owners * rows, cols)
        r = dot(h_ref[...], w)
        for k in range(tiles):
            o_ref[:, k] = r[:, k * 128 : (k + 1) * 128].reshape(length // 8, 8, 128)

    return pl.pallas_call(
        body,
        grid=(blocks,),
        out_shape=jax.ShapeDtypeStruct((length // 8, inner // 128, 8, 128), F32),
        in_specs=[
            pl.BlockSpec(hidden.shape, lambda b: (0, 0)),
            pl.BlockSpec((1, owners, rows, cols), lambda b: (b, 0, 0, 0)),
        ],
        out_specs=pl.BlockSpec((length // 8, tiles, 8, 128), lambda b: (0, b, 0, 0)),
        compiler_params=pltpu.CompilerParams(vmem_limit_bytes=40 << 20),
        cost_estimate=pl.CostEstimate(
            flops=2 * length * hidden.shape[1] * inner,
            bytes_accessed=2 * hidden.shape[1] * inner + 4 * length * inner,
            transcendentals=0,
        ),
        name="project",
    )(hidden, weight)


def mixer_forward(keep, bound, x, x_proj, dt_proj, params, decay2, *, tokens, inner, states, rank, taps, slots):
    blocks, tiles, octets = inner // 1024, inner // 128, tokens // 8
    size = octets // slots
    rows = tokens * tiles

    def body(keep_ref, bound_ref, x_ref, xw_ref, dt_ref, p_ref, a_ref, y_ref, sf_ref, sr_ref, df_ref, dr_ref, proj_ref, bc_ref):
        shape4 = (octets, tiles, 8, 128)
        y4 = y_ref.reshape(shape4)
        s4 = (sf_ref.reshape(shape4), sr_ref.reshape(shape4))
        d4 = (df_ref.reshape(shape4), dr_ref.reshape(shape4))

        def conv(k, _):
            p = p_ref[k]
            skip = p[taps + 2 : taps + 3][None]
            for q in range(slots):
                both, _ = convolved(extended(x_ref, k, q, size, bound_ref, slots), p, taps)
                sl = pl.ds(q * size, size)
                series = [c * jax.nn.sigmoid(c) for c in both]
                for ref, v in zip(s4, series):
                    ref[sl, k] = v
                y4[sl, k] = skip * (series[0] + series[1])
            return 0

        lax.fori_loop(0, tiles, conv, 0)
        lanes = lax.broadcasted_iota(jnp.int32, (tokens, 128), 1)
        for s in range(2):
            total = jnp.zeros((tokens, 128), F32)
            for k in range(0, tiles, 2):
                lhs = jnp.concatenate(
                    [s4[s][:, k + i].reshape(tokens, 128).astype(BF16) for i in range(2)], axis=1
                )
                total = total + dot(lhs, xw_ref[pl.ds(k * 128, 256), :])
            proj_ref[s] = total
            low = jnp.where(lanes < rank, total, 0.0).astype(BF16)
            for k in range(0, tiles, 2):
                pre = dot_nt(low, dt_ref[pl.ds(k * 128, 256), :])
                for i in range(2):
                    v = pre[:, i * 128 : (i + 1) * 128] + p_ref[k + i, taps + 1 : taps + 2, :]
                    step = jnp.maximum(v, 0.0) + jnp.log1p(jnp.exp(-jnp.abs(v)))
                    d4[s][:, k + i] = step.reshape(octets, 8, 128)
        for s, (d_ref, u_ref) in enumerate(((df_ref, sf_ref), (dr_ref, sr_ref))):
            rev = s == 1
            for ng in range(states // GROUP):
                fill_columns(proj_ref.at[s], bc_ref, tokens, rank, ng, states)
                a = [
                    [a_ref[pl.ds((ng * GROUP + n) * tiles + c * 8, 8), :] for c in range(blocks)]
                    for n in range(GROUP)
                ]

                def octet(i, hs):
                    g = (octets - 1 - i) if rev else i
                    keep_now = keep_ref[s, i]
                    hs = [h * keep_now for h in hs]
                    base = pl.multiple_of(g * (tiles * 8), 8)
                    for j in range(8):
                        tt = 7 - j if rev else j
                        t = g * 8 + tt
                        for c in range(blocks):
                            sl = pl.ds(base + c * 64 + tt, 8, stride=8)
                            d = d_ref[sl, :]
                            du = d * u_ref[sl, :]
                            acc = None
                            for n in range(GROUP):
                                b = bc_ref[pl.ds(n * tokens + t, 1), :]
                                cc = bc_ref[pl.ds((GROUP + n) * tokens + t, 1), :]
                                k = n * blocks + c
                                hs[k] = jnp.exp2(d * a[n][c]) * hs[k] + du * b
                                acc = hs[k] * cc if acc is None else acc + hs[k] * cc
                            y_ref[sl, :] = y_ref[sl, :] + acc
                    return hs

                lax.fori_loop(0, octets, octet, [jnp.zeros((8, 128), F32)] * (GROUP * blocks))

    big = jax.ShapeDtypeStruct((rows, 128), F32)
    return pl.pallas_call(
        body,
        out_shape=(big,) * 5 + (jax.ShapeDtypeStruct((2, tokens, 128), F32),),
        in_specs=[SMEM, SMEM] + [VMEM] * 5,
        out_specs=(VMEM,) * 6,
        scratch_shapes=[pltpu.VMEM((2 * GROUP * tokens, 128), F32)],
        compiler_params=pltpu.CompilerParams(vmem_limit_bytes=56 << 20),
        cost_estimate=pl.CostEstimate(
            flops=tokens * inner * states * 160,
            bytes_accessed=6 * rows * 512,
            transcendentals=2 * tokens * inner * states,
        ),
        name="mixer_forward",
    )(keep, bound, x, x_proj, dt_proj, params, decay2)


def mixer_middle(place, hidden, weight, out_weight, branch_grad, total, *, rows, length, inner):
    blocks, owners, _, cols = weight.shape[0], weight.shape[1], 0, weight.shape[-1]
    packed = out_weight is None
    dp, per, wide = branch_grad.shape[0], owners // blocks, branch_grad.shape[2]
    tiles, octets = cols // 128, length // 8
    half = rows
    width = hidden.shape[1]

    def body(place_ref, h_ref, wz_ref, wo_ref, bg_ref, t_ref, g_ref, dz_ref, br_ref, *more):
        ml_ref, gz_ref, go_ref, ht_ref, sem = more[-5:]
        b = pl.program_id(0)
        where = place_ref[b]

        def copies():
            if packed:
                return [
                    pltpu.make_async_copy(gz_ref, more[0].at[b, :, 0], sem.at[0]),
                    pltpu.make_async_copy(go_ref, more[0].at[:, pl.ds(where * per, per), 1], sem.at[1]),
                ]
            return [
                pltpu.make_async_copy(gz_ref, more[0].at[b], sem.at[0]),
                pltpu.make_async_copy(go_ref, more[1].at[:, pl.ds(where * per, per)], sem.at[1]),
            ]

        z = dot(h_ref[...], wz_ref[...].reshape(owners * rows, cols))

        def out_rows(d):
            if not packed:
                return wo_ref[d].reshape(cols, wide)
            pieces = []
            for j in range(per):
                for i in range(2):
                    pieces.append(wo_ref[d, j, 0, :, i * wide : (i + 1) * wide])
            return jnp.concatenate(pieces, axis=0)

        mg = dot_nt(bg_ref[0], out_rows(0))
        for d in range(1, dp):
            mg = mg + dot_nt(bg_ref[d], out_rows(d))
        for k in range(tiles):
            sl = slice(k * 128, (k + 1) * 128)
            zk, mk, tk = z[:, sl], mg[:, sl], t_ref[:, k].reshape(length, 128)
            gate = jax.nn.sigmoid(zk)
            silu = zk * gate
            ml_ref[:, sl] = (tk * silu).astype(BF16)
            g_ref[:, k] = (mk * silu).reshape(octets, 8, 128)
            dz_ref[:, sl] = (mk * tk * (gate * (1.0 + zk * (1.0 - gate)))).astype(BF16)
        ml = ml_ref[...]
        ml_t = ml.T

        @pl.when(b == 0)
        def _():
            br_ref[...] = jnp.zeros_like(br_ref)
            ht_ref[...] = h_ref[...].T

        @pl.when(b > 0)
        def _():
            for c in copies():
                c.wait()

        for d in range(dp):
            br_ref[d] = br_ref[d] + dot(ml, out_rows(d))
            go = dot(ml_t, bg_ref[d]).astype(BF16)
            if packed:
                at = 0
                for j in range(per):
                    for i in range(2):
                        go_ref[d, j, :, i * wide : (i + 1) * wide] = go[at : at + half]
                        at += half
            else:
                go_ref[d] = go.reshape(go_ref.shape[1:])
        gz_ref[...] = dot(ht_ref[...], dz_ref[...]).astype(BF16).reshape(owners, rows, cols)
        for c in copies():
            c.start()

        @pl.when(b == blocks - 1)
        def _():
            for c in copies():
                c.wait()

    if packed:
        wz_spec = pl.BlockSpec((1, owners, 1, rows, cols), lambda b, p: (b, 0, 0, 0, 0))
        wo_spec = pl.BlockSpec((dp, per, 1, rows, cols), lambda b, p: (0, p[b], 1, 0, 0))
        extra = (jax.ShapeDtypeStruct((blocks, owners, 2, rows, cols), BF16),)
        go_shape = (dp, per, rows, cols)
        out_weight = weight
    else:
        wz_spec = pl.BlockSpec((1, owners, rows, cols), lambda b, p: (b, 0, 0, 0))
        wo_spec = pl.BlockSpec((dp, per, 2 * rows, wide), lambda b, p: (0, p[b], 0, 0))
        extra = (
            jax.ShapeDtypeStruct((blocks, owners, rows, cols), BF16),
            jax.ShapeDtypeStruct((dp, owners, 2 * rows, wide), BF16),
        )
        go_shape = (dp, per, 2 * rows, wide)
    whole = lambda v: pl.BlockSpec(v.shape, lambda b, p: (0,) * v.ndim)
    tile_spec = pl.BlockSpec((octets, tiles, 8, 128), lambda b, p: (0, b, 0, 0))
    return pl.pallas_call(
        body,
        grid_spec=pltpu.PrefetchScalarGridSpec(
            num_scalar_prefetch=1,
            grid=(blocks,),
            in_specs=[
                whole(hidden),
                wz_spec,
                wo_spec,
                whole(branch_grad),
                tile_spec,
            ],
            out_specs=(
                tile_spec,
                pl.BlockSpec((length, cols), lambda b, p: (0, b)),
                pl.BlockSpec((dp, length, wide), lambda b, p: (0, 0, 0)),
            )
            + (ANY,) * len(extra),
            scratch_shapes=[
                pltpu.VMEM((length, cols), BF16),
                pltpu.VMEM((owners, rows, cols), BF16),
                pltpu.VMEM(go_shape, BF16),
                pltpu.VMEM((width, length), BF16),
                pltpu.SemaphoreType.DMA((2,)),
            ],
        ),
        out_shape=(
            jax.ShapeDtypeStruct((octets, inner // 128, 8, 128), F32),
            jax.ShapeDtypeStruct((length, inner), BF16),
            jax.ShapeDtypeStruct((dp, length, wide), F32),
        )
        + extra,
        compiler_params=pltpu.CompilerParams(vmem_limit_bytes=56 << 20),
        cost_estimate=pl.CostEstimate(
            flops=10 * length * width * inner, bytes_accessed=60 << 20, transcendentals=length * inner
        ),
        name="mixer_middle",
    )(place, hidden, weight, out_weight, branch_grad, total)


def mixer_backward(keep, proj, step, series, grad, decay2, x_proj, dt_proj, params, *, rev, tokens, inner, states, rank, taps):
    blocks, tiles, octets = inner // 1024, inner // 128, tokens // 8
    slots = GROUP * blocks
    rows = tokens * tiles

    def body(
        keep_ref, proj_ref, d_ref, u_ref, g_ref, a_ref, xw_ref, dt_ref, p_ref,
        ddu_ref, small_ref, da_ref, skip_ref,
        dd_ref, bc_ref, h_ref, r_ref, cols_ref,
    ):
        zero = jnp.zeros((8, 128), F32)
        cols_ref[...] = jnp.zeros_like(cols_ref)
        for ng in range(states // GROUP):
            fill_columns(proj_ref, bc_ref, tokens, rank, ng, states)
            a = [
                [a_ref[pl.ds((ng * GROUP + n) * tiles + c * 8, 8), :] for c in range(blocks)]
                for n in range(GROUP)
            ]
            for k in range(slots):
                h_ref[pl.ds(k * 8, 8), :] = zero

            def ahead(i, hs):
                g = (octets - 1 - i) if rev else i
                keep_now = keep_ref[i]
                hs = [h * keep_now for h in hs]
                base = pl.multiple_of(g * (tiles * 8), 8)
                for j in range(8):
                    tt = 7 - j if rev else j
                    t = g * 8 + tt
                    hb = pl.multiple_of((i * 8 + j + 1) * (slots * 8), 8)
                    for c in range(blocks):
                        sl = pl.ds(base + c * 64 + tt, 8, stride=8)
                        d = d_ref[sl, :]
                        du = d * u_ref[sl, :]
                        for n in range(GROUP):
                            b = bc_ref[pl.ds(n * tokens + t, 1), :]
                            k = n * blocks + c
                            hs[k] = jnp.exp2(d * a[n][c]) * hs[k] + du * b
                            h_ref[pl.ds(hb + k * 8, 8), :] = hs[k]
                return hs

            lax.fori_loop(0, octets, ahead, [zero] * slots)

            def back(ii, carry):
                gs, das = [list(v) for v in carry]
                i = octets - 1 - ii
                g = (octets - 1 - i) if rev else i
                keep_now = keep_ref[i]
                base = pl.multiple_of(g * (tiles * 8), 8)
                for jj in range(8):
                    j = 7 - jj
                    tt = 7 - j if rev else j
                    t = g * 8 + tt
                    hb = pl.multiple_of((i * 8 + j) * (slots * 8), 8)
                    pb, pc = [None] * GROUP, [None] * GROUP
                    for c in range(blocks):
                        sl = pl.ds(base + c * 64 + tt, 8, stride=8)
                        d = d_ref[sl, :]
                        du = d * u_ref[sl, :]
                        gy = g_ref[sl, :]
                        ddu = dd = None
                        for n in range(GROUP):
                            b = bc_ref[pl.ds(n * tokens + t, 1), :]
                            cc = bc_ref[pl.ds((GROUP + n) * tokens + t, 1), :]
                            k = n * blocks + c
                            before = h_ref[pl.ds(hb + k * 8, 8), :]
                            after = h_ref[pl.ds(hb + (slots + k) * 8, 8), :]
                            adj = gs[k] + cc * gy
                            x = after * gy
                            pc[n] = x if c == 0 else pc[n] + x
                            x = adj * du
                            pb[n] = x if c == 0 else pb[n] + x
                            x = adj * b
                            ddu = x if n == 0 else ddu + x
                            moved = adj * jnp.exp2(d * a[n][c])
                            if j == 0:
                                moved = moved * keep_now
                            gs[k] = moved
                            m = moved * before
                            x = m * a[n][c]
                            dd = x if n == 0 else dd + x
                            das[k] = das[k] + m * d
                        if ng == 0:
                            ddu_ref[sl, :] = ddu
                            dd_ref[sl, :] = dd
                        else:
                            ddu_ref[sl, :] = ddu_ref[sl, :] + ddu
                            dd_ref[sl, :] = dd_ref[sl, :] + dd
                    r_ref[pl.ds(pl.multiple_of(t * 8, 8), 8), :] = sublane_sums(pb + pc)
                return gs, das

            _, das = lax.fori_loop(0, octets, back, ([zero] * slots, [zero] * slots))
            for n in range(GROUP):
                for c in range(blocks):
                    da_ref[pl.ds((ng * GROUP + n) * tiles + c * 8, 8), :] = das[n * blocks + c]
            lane = lax.broadcasted_iota(jnp.int32, (128, 128), 1)
            for q in range(2 * GROUP):
                col = rank + (q // GROUP) * states + ng * GROUP + q % GROUP
                one = jnp.where(lane == col, 1.0, 0.0).astype(BF16)
                v = r_ref[pl.ds(q, tokens, stride=8), :]
                high_part = v.astype(BF16)
                low_part = (v - high_part.astype(F32)).astype(BF16)
                cols_ref[...] += dot(high_part, one) + dot(low_part, one)
        shape4 = (octets, tiles, 8, 128)
        d4, u4, g4, ddu4, dd4 = [r.reshape(shape4) for r in (d_ref, u_ref, g_ref, ddu_ref, dd_ref)]
        lanes = lax.broadcasted_iota(jnp.int32, (tokens, 128), 1)
        low = jnp.where(lanes < rank, proj_ref[...], jnp.where(lanes == rank, 1.0, 0.0)).astype(BF16)
        low_t = low.T
        proj_grad = jnp.zeros((tokens, 128), F32)
        for k in range(0, tiles, 2):
            pair = []
            for i in range(2):
                d, u, gy, ddu = d4[:, k + i], u4[:, k + i], g4[:, k + i], ddu4[:, k + i]
                pre = (ddu * u + LN2 * dd4[:, k + i]) * (1.0 - jnp.exp(-d))
                pair.append(pre.reshape(tokens, 128).astype(BF16))
                ddu4[:, k + i] = ddu * d + p_ref[k + i, taps + 2 : taps + 3, :][None] * gy
                skip_ref[k + i] = jnp.sum(gy * u, axis=0)
            pre = jnp.concatenate(pair, axis=1)
            proj_grad = proj_grad + dot(pre, dt_ref[pl.ds(k * 128, 256), :])
            small_ref[128:256, k * 128 : (k + 2) * 128] = dot(low_t, pre)
        proj_grad = jnp.where(lanes < rank, proj_grad, cols_ref[...]).astype(BF16)
        proj_t = proj_grad.T
        for k in range(0, tiles, 2):
            pair = [u4[:, k + i].reshape(tokens, 128).astype(BF16) for i in range(2)]
            small_ref[0:128, k * 128 : (k + 2) * 128] = dot(proj_t, jnp.concatenate(pair, axis=1))
            more = dot_nt(proj_grad, xw_ref[pl.ds(k * 128, 256), :])
            for i in range(2):
                ddu4[:, k + i] = ddu4[:, k + i] + more[:, i * 128 : (i + 1) * 128].reshape(octets, 8, 128)

    return pl.pallas_call(
        body,
        out_shape=(
            jax.ShapeDtypeStruct((rows, 128), F32),
            jax.ShapeDtypeStruct((256, inner), F32),
            jax.ShapeDtypeStruct((states * tiles, 128), F32),
            jax.ShapeDtypeStruct((tiles, 8, 128), F32),
        ),
        in_specs=[SMEM] + [VMEM] * 8,
        out_specs=(VMEM,) * 4,
        scratch_shapes=[
            pltpu.VMEM((rows, 128), F32),
            pltpu.VMEM((2 * GROUP * tokens, 128), F32),
            pltpu.VMEM((slots * 8 * (tokens + 1), 128), F32),
            pltpu.VMEM((tokens * 8, 128), F32),
            pltpu.VMEM((tokens, 128), F32),
        ],
        compiler_params=pltpu.CompilerParams(vmem_limit_bytes=60 << 20),
        cost_estimate=pl.CostEstimate(
            flops=tokens * inner * states * 160,
            bytes_accessed=5 * rows * 512,
            transcendentals=2 * tokens * inner * states,
        ),
        name="mixer_backward",
    )(keep, proj, step, series, grad, decay2, x_proj, dt_proj, params)


def mixer_finish(place, bound, x, grads, params, hidden, *, rows, cols, owners, length, inner, taps, slots):
    blocks = inner // cols
    tiles, octets = cols // 128, length // 8
    size = octets // slots
    width = hidden.shape[1]
    cores = 2
    fz = owners // cores

    def body(place_ref, bound_ref, x_ref, gf_ref, gr_ref, p_ref, h_ref, mine_ref, twin_ref, dx_ref, gw_ref, cf_ref, cr_ref, ht_ref):
        def first(k, _):
            p = p_ref[k]
            sums = [jnp.zeros((8, 128), F32) for _ in range(taps + 1)]
            for q in range(slots):
                ext = extended(x_ref, k, q, size, bound_ref, slots)
                both, moves = convolved(ext, p, taps)
                sl = pl.ds(q * size, size)
                for s, (c, src, dst) in enumerate(zip(both, (gf_ref, gr_ref), (cf_ref, cr_ref))):
                    gate = jax.nn.sigmoid(c)
                    dc = src[sl, k] * (gate * (1.0 + c * (1.0 - gate)))
                    dst[sl, k] = dc
                    sums[taps] = sums[taps] + jnp.sum(dc, axis=0)
                    sums[taps - 1] = sums[taps - 1] + jnp.sum(dc * ext[1:-1], axis=0)
                    for j in range(1, taps):
                        m = moves[s * (taps - 1) + j - 1]
                        sums[taps - 1 - j] = sums[taps - 1 - j] + jnp.sum(dc * m, axis=0)
            for i, v in enumerate(sums):
                gw_ref[k, i] = v
            return 0

        @pl.when(pl.program_id(0) == 0)
        def _():
            ht = h_ref[...].T
            for j in range(owners):
                at = ((j % cores) ^ place_ref[2]) * fz + ((j // cores) ^ place_ref[1])
                ht_ref[pl.ds(pl.multiple_of(at * rows, 16), rows), :] = ht[j * rows : (j + 1) * rows]

        lax.fori_loop(0, tiles, first, 0)
        for k in range(tiles):
            p = p_ref[k]
            for q in range(slots):
                ef = extended(cf_ref, k, q, size, bound_ref, slots)
                er = extended(cr_ref, k, q, size, bound_ref, slots)
                v = p[taps - 1 : taps][None] * (ef[1:-1] + er[1:-1])
                for j in range(1, taps):
                    v = v + p[taps - 1 - j : taps - j][None] * (shifted(ef, j, True) + shifted(er, j, False))
                dx_ref[pl.ds(q * size * 8, size * 8), k * 128 : (k + 1) * 128] = v.reshape(size * 8, 128).astype(BF16)
        dx = dx_ref[...]
        gx = dot(ht_ref[...], dx).astype(BF16).reshape(cores, fz, rows, cols)
        mine_ref[:, 0] = gx[0]
        twin_ref[:, 0] = gx[1]

    tile_spec = pl.BlockSpec((octets, tiles, 8, 128), lambda b, p: (0, b, 0, 0))
    part_spec = pl.BlockSpec((fz, 1, rows, cols), lambda b, p: (0, b ^ p[0], 0, 0))
    part = jax.ShapeDtypeStruct((fz, blocks, rows, cols), BF16)
    return pl.pallas_call(
        body,
        grid_spec=pltpu.PrefetchScalarGridSpec(
            num_scalar_prefetch=1,
            grid=(blocks,),
            in_specs=[
                SMEM,
                tile_spec,
                tile_spec,
                tile_spec,
                pl.BlockSpec((tiles, 8, 128), lambda b, p: (b, 0, 0)),
                pl.BlockSpec(hidden.shape, lambda b, p: (0, 0)),
            ],
            out_specs=(
                part_spec,
                part_spec,
                pl.BlockSpec((length, cols), lambda b, p: (0, b)),
                pl.BlockSpec((tiles, taps + 1, 8, 128), lambda b, p: (b, 0, 0, 0)),
            ),
            scratch_shapes=[
                pltpu.VMEM((octets, tiles, 8, 128), F32),
                pltpu.VMEM((octets, tiles, 8, 128), F32),
                pltpu.VMEM((width, length), BF16),
            ],
        ),
        out_shape=(
            part,
            part,
            jax.ShapeDtypeStruct((length, inner), BF16),
            jax.ShapeDtypeStruct((inner // 128, taps + 1, 8, 128), F32),
        ),
        compiler_params=pltpu.CompilerParams(vmem_limit_bytes=56 << 20),
        cost_estimate=pl.CostEstimate(
            flops=2 * length * width * inner, bytes_accessed=30 << 20, transcendentals=2 * length * inner
        ),
        name="mixer_finish",
    )(place, bound, x, grads[0], grads[1], params, hidden)


def hidden_back(x_grad, z_grad, wx, wz, *, rows):
    blocks, owners, cols = wx.shape[0], wx.shape[1], wx.shape[-1]
    length, width = x_grad.shape[0], owners * rows

    def body(dx_ref, dz_ref, wx_ref, wz_ref, hg_ref):
        hg = dot_nt(dx_ref[...], wx_ref[...].reshape(width, cols)) + dot_nt(
            dz_ref[...], wz_ref[...].reshape(width, cols)
        )

        @pl.when(pl.program_id(0) == 0)
        def _():
            hg_ref[...] = hg

        @pl.when(pl.program_id(0) > 0)
        def _():
            hg_ref[...] = hg_ref[...] + hg

    w_spec = pl.BlockSpec((1, owners, rows, cols), lambda b: (b, 0, 0, 0))
    z_spec = pl.BlockSpec((1, owners, 1, rows, cols), lambda b: (b, 0, 0, 0, 0)) if wz.ndim == 5 else w_spec
    return pl.pallas_call(
        body,
        grid=(blocks,),
        in_specs=[pl.BlockSpec((length, cols), lambda b: (0, b))] * 2 + [w_spec, z_spec],
        out_specs=pl.BlockSpec((length, width), lambda b: (0, 0)),
        out_shape=jax.ShapeDtypeStruct((length, width), F32),
        compiler_params=pltpu.CompilerParams(vmem_limit_bytes=40 << 20),
        cost_estimate=pl.CostEstimate(
            flops=4 * length * width * blocks * cols, bytes_accessed=24 << 20, transcendentals=0
        ),
        name="hidden_back",
    )(x_grad, z_grad, wx, wz)


def swap(v, axis, k):
    return lax.ppermute(v, axis, [(i, i ^ k) for i in range(lax.axis_size(axis))])


def others(v, axis):
    return jnp.stack([v] + [swap(v, axis, k) for k in range(1, lax.axis_size(axis))])


def gather_all(v):
    return others(others(others(v, "fz"), "dp"), "core")


def added(v, axis, dim):
    parts = [lax.index_in_dim(v, k, dim, keepdims=False) for k in range(lax.axis_size(axis))]
    return sum((swap(p, axis, k) if k else p).astype(F32) for k, p in enumerate(parts))


def relative(v, dim, me):
    n = v.shape[dim]
    return jnp.concatenate([lax.dynamic_slice_in_dim(v, me ^ k, 1, axis=dim) for k in range(n)], axis=dim)


def per_device(
    tokens,
    segment,
    timestep,
    ada_weight,
    ada_bias,
    in_weight,
    conv_weight,
    convolution_bias,
    xproj_weight,
    dtproj_weight,
    dt_bias,
    a_log,
    d_skip,
    out_weight,
    cotangent,
):
    dp, fz, cores = [lax.axis_size(n) for n in ALL]
    my_dp = lax.axis_index("dp")
    my_j = lax.axis_index("fz") * cores + lax.axis_index("core")
    fsdp = fz * cores
    devices = dp * fsdp
    slots = timestep.shape[0]
    length, width = tokens.shape
    taps, rank, states = conv_weight.shape[1], dtproj_weight.shape[1], a_log.shape[1]
    own = conv_weight.shape[0]
    inner = own * devices
    rows, cols = in_weight.shape[0], in_weight.shape[1] // 2
    wide = out_weight.shape[1]
    packs = wide % 128 == 0
    contract_rows = (((0,), (0,)), ((), ()))

    lower = my_dp < dp // 2
    opposite = [(i, (i + dp // 2) % dp) for i in range(dp)]
    left, right = in_weight[:, :cols], in_weight[:, cols:]
    got = lax.ppermute(jnp.where(lower, right, left), "dp", opposite)
    kept = jnp.where(lower, left, right)
    x_cols, z_cols = jnp.where(lower, kept, got), jnp.where(lower, got, kept)
    order = [(b % (dp // 2)) * 2 + b // (dp // 2) for b in range(dp)]

    parts = [
        xproj_weight,
        dtproj_weight,
        conv_weight,
        convolution_bias[:, None],
        dt_bias[:, None],
        d_skip[:, None],
        a_log,
    ]
    packed = jnp.concatenate(parts, axis=1)
    packed = jnp.pad(packed, ((0, 0), (0, 256 - packed.shape[1])))
    tail = own * 256 // cols
    g_x = lax.all_gather(jnp.concatenate([x_cols, packed.reshape(tail, cols)], axis=0), ALL, axis=0, tiled=True)
    g_x = g_x.reshape(dp, fsdp, rows + tail, cols)
    times = gather_all(timestep).reshape(-1)
    ada_rows, ada_cols = ada_weight.shape
    condition = embed_columns(
        times, my_j * ada_rows + jnp.arange(ada_rows, dtype=jnp.int32), width
    ).astype(BF16)
    bias_cols = ada_bias.shape[0]
    bias_part = lax.dynamic_update_slice(
        jnp.zeros((ada_cols,), F32), ada_bias.astype(F32), (my_j * bias_cols,)
    )
    partial = jnp.dot(condition, ada_weight, preferred_element_type=F32) + bias_part[None, :]
    partial = partial.reshape(cores, dp, fz, slots, ada_cols)
    partial = partial[0] + swap(partial[1], "core", 1)
    partial = partial[:, 0] + sum(swap(partial[:, k], "fz", k) for k in range(1, fz))
    blocks = jnp.stack([partial[0]] + [swap(partial[k], "dp", k) for k in range(1, dp)])
    modulation = jnp.concatenate(
        [lax.dynamic_index_in_dim(blocks, my_dp ^ b, keepdims=False) for b in range(dp)], axis=1
    )
    picker = (segment[:, None] == jnp.arange(slots, dtype=jnp.int32)[None, :]).astype(F32)
    per_token = jnp.dot(picker, modulation, precision=high)
    shift_mod = per_token[:, :width]
    scale_mod = per_token[:, width : 2 * width]
    gate_mod = per_token[:, 2 * width :]
    centered = tokens - jnp.mean(tokens, axis=1, keepdims=True)
    inv_std = lax.rsqrt(jnp.mean(centered * centered, axis=1, keepdims=True) + 1e-06)
    normed = centered * inv_std
    hidden = (normed * (1.0 + scale_mod) + shift_mod).astype(BF16)
    branch_grad = (cotangent * gate_mod).astype(BF16)
    branch_grad = branch_grad.reshape(length, dp, wide).transpose(1, 0, 2)

    if packs:
        out_piece = jnp.concatenate([out_weight[:rows], out_weight[rows:]], axis=1)
        later = jnp.stack([z_cols, out_piece])
        later, g_x, hidden = lax.optimization_barrier((later, g_x, hidden))
        g_z = lax.all_gather(later, ALL, axis=0, tiled=True).reshape(dp, fsdp, 2, rows, cols)
        g_out = None
    else:
        g_z = lax.all_gather(z_cols, ALL, axis=0, tiled=True).reshape(dp, fsdp, rows, cols)
        g_out = lax.all_gather(out_weight, ALL, axis=0, tiled=True).reshape(dp, fsdp, 2 * rows, wide)

    packed = g_x[:, :, rows:, :].reshape(dp, inner // dp, 256)
    packed = jnp.concatenate([packed[o] for o in order], axis=0)
    x_proj, dt_proj = packed[:, :128], packed[:, 128:256]
    rest = packed[:, 128 + rank :].astype(F32).T
    params = rest[:8].reshape(8, inner // 128, 128).transpose(1, 0, 2)
    decay = -jnp.exp(rest[taps + 3 : taps + 3 + states])
    decay2 = (decay * (1.0 / LN2)).reshape(states * inner // 128, 128)

    same = (segment[1:] == segment[:-1]).astype(F32)
    same = jnp.concatenate([jnp.zeros((1,), F32), same, jnp.zeros((1,), F32)])
    keep_f, keep_r = same[0:length:8], same[8 : length + 1 : 8][::-1]
    bound = same[0 : length : length // slots]
    sizes = dict(tokens=length, inner=inner, states=states, rank=rank, taps=taps)

    x = project(hidden, g_x, rows=rows, length=length, inner=inner)
    total, series_f, series_r, step_f, step_r, proj = mixer_forward(
        jnp.stack([keep_f, keep_r]), bound, x, x_proj, dt_proj, params, decay2, slots=slots, **sizes
    )
    tile_shape = (length // 8, inner // 128, 8, 128)
    middle = mixer_middle(
        jnp.asarray(order, jnp.int32),
        hidden,
        g_z,
        g_out,
        branch_grad,
        total.reshape(tile_shape),
        rows=rows,
        length=length,
        inner=inner,
    )
    grad, z_grad, branch = middle[:3]
    branch = branch.transpose(1, 0, 2).reshape(length, width)
    layer_out = tokens + gate_mod * branch
    gate_grad = cotangent * branch

    def scattered(v):
        return lax.psum_scatter(v.reshape(-1, v.shape[-1]), ALL, scatter_dimension=0, tiled=True)

    if packs:
        early = scattered(middle[3])
        z_shard, out_shard = early[:rows], early[rows:]
        out_shard = jnp.concatenate([out_shard[:, :wide], out_shard[:, wide:]], axis=0)
    else:
        z_shard, out_shard = early = scattered(middle[3]), scattered(middle[4])

    grad = grad.reshape(total.shape)
    series_grad, small, da, skip_part = [], 0.0, 0.0, 0.0
    for k, (keep, step, series) in enumerate(((keep_f, step_f, series_f), (keep_r, step_r, series_r))):
        got = mixer_backward(
            keep, proj[k], step, series, grad, decay2, x_proj, dt_proj, params, rev=k == 1, **sizes
        )
        series_grad.append(got[0].reshape(tile_shape))
        small, da, skip_part = small + got[1], da + got[2], skip_part + got[3]

    my_place = jnp.stack([lax.axis_index(n) for n in ALL]).astype(jnp.int32)
    mine, twin, x_grad, conv_part = mixer_finish(
        my_place,
        bound,
        x,
        series_grad,
        params,
        hidden,
        rows=rows,
        cols=cols,
        owners=fsdp,
        length=length,
        inner=inner,
        taps=taps,
        slots=slots,
    )
    small_t = jnp.concatenate(
        [
            small[: 128 + rank + 1],
            skip_part.sum(axis=1).reshape(1, inner),
            da.reshape(states, inner) * decay,
            jnp.zeros((256 - 128 - rank - 2 - states, inner), F32),
        ],
        axis=0,
    ).astype(BF16)
    small = small_t.T.reshape(dp, inner // dp, 256)
    small = jnp.concatenate([small[order.index(o)] for o in range(dp)], axis=0)
    cut = cols // 3 // 128 * 128
    extra = own * 256 // (cols - cut)
    small = small.reshape(dp, fz, cores, extra, cols - cut)
    for dim, axis in enumerate(ALL):
        small = relative(small, dim, lax.axis_index(axis))
    small_twin = swap(small[:, :, 1], "core", 1)
    other = swap(twin, "core", 1)

    def both(k, first):
        if first:
            a, b = [v[k, :, :, :cut].astype(F32) for v in (mine, other)]
            return a + b
        a, b = [v[:, k, :, cut:].astype(F32) for v in (mine, other)]
        return jnp.concatenate([a + b, small[k, :, 0].astype(F32) + small_twin[k].astype(F32)], axis=1)

    sends = [[both(k, first).astype(BF16) for k in range(1, n)] for first, n in ((True, fz), (False, dp))]
    sends, x_grad, _ = lax.optimization_barrier((sends, x_grad, early))
    arrived = [[swap(v, axis, k + 1) for k, v in enumerate(send)] for send, axis in zip(sends, ("fz", "dp"))]
    arrived[0][0], x_grad = lax.optimization_barrier((arrived[0][0], x_grad))
    x_first, x_second = [
        (both(0, first) + sum(v.astype(F32) for v in got)).astype(BF16) for first, got in zip((True, False), arrived)
    ]
    hidden_grad = hidden_back(x_grad, z_grad, g_x, g_z, rows=rows)

    normed_grad = hidden_grad * (1.0 + scale_mod)
    grad_tokens = cotangent + inv_std * (
        normed_grad
        - jnp.mean(normed_grad, axis=1, keepdims=True)
        - normed * jnp.mean(normed_grad * normed, axis=1, keepdims=True)
    )
    token_mod_grad = jnp.concatenate([hidden_grad, hidden_grad * normed, gate_grad], axis=1)
    mod_low = lax.dot_general(picker, token_mod_grad, contract_rows, precision=high).astype(BF16)
    valid = (segment < slots).astype(F32)[:, None]
    sums = jnp.stack(
        [
            jnp.sum(layer_out * layer_out * valid),
            jnp.sum(grad_tokens * grad_tokens * valid),
            jnp.sum(valid) * width,
        ]
    )
    pieces, rest = [], sums
    for _ in range(3):
        pieces.append(lax.optimization_barrier(rest.astype(BF16)))
        rest = rest - pieces[-1].astype(F32)
    pieces = jnp.pad(jnp.concatenate(pieces)[None, :], ((0, slots - 1), (0, 128 - 9)))
    conv_rows = conv_part.sum(axis=2).transpose(1, 0, 2).reshape((taps + 1) * inner)
    conv_cols = -(-conv_rows.shape[0] // (slots * 128)) * 128
    conv_rows = jnp.pad(conv_rows, (0, slots * conv_cols - conv_rows.shape[0]))
    mod_low = jnp.concatenate([mod_low, pieces, conv_rows.reshape(slots, conv_cols).astype(BF16)], axis=1)
    mod_all = gather_all(mod_low).reshape(devices * slots, -1)
    row = jnp.arange(devices * slots, dtype=jnp.int32) % slots
    slot_rows = (row[None, :] == jnp.arange(slots, dtype=jnp.int32)[:, None]).astype(BF16)
    conv_grad = jnp.dot(slot_rows, mod_all[:, dp * ada_cols + 128 :], preferred_element_type=F32)
    conv_grad = conv_grad.reshape(-1)[: (taps + 1) * inner].reshape(taps + 1, dp, inner // dp)
    conv_grad = jnp.stack([conv_grad[:, order.index(o)] for o in range(dp)], axis=1).reshape(taps + 1, inner)
    conv_grad = lax.dynamic_slice_in_dim(conv_grad, (my_dp * fsdp + my_j) * own, own, axis=1).T
    mod_cols = lax.dynamic_slice_in_dim(mod_all, my_dp * ada_cols, ada_cols, axis=1)
    grad_ada_w = lax.dot_general(condition, mod_cols, contract_rows, preferred_element_type=F32)
    grad_ada_b = jnp.sum(
        lax.dynamic_slice_in_dim(mod_cols, my_j * bias_cols, bias_cols, axis=1).astype(F32), axis=0
    )
    sums = jnp.sum(mod_all[:, dp * ada_cols : dp * ada_cols + 9].astype(F32), axis=0)
    out_sq, grad_sq, counted = [sums[i] + sums[i + 3] + sums[i + 6] for i in range(3)]
    x_second = added(x_second, "fz", 0)
    small = x_second[rows:].reshape(own, 256)
    x_shard = jnp.concatenate([added(x_first, "dp", 0), x_second[:rows]], axis=1).astype(BF16)
    got = lax.ppermute(jnp.where(lower, z_shard, x_shard), "dp", opposite)
    grad_in_shard = jnp.where(
        lower,
        jnp.concatenate([x_shard, got], axis=1),
        jnp.concatenate([got, z_shard], axis=1),
    ).astype(F32)
    at = 128 + rank
    return (
        layer_out,
        grad_tokens,
        grad_ada_w,
        grad_ada_b,
        grad_in_shard,
        conv_grad[:, :taps],
        conv_grad[:, taps],
        small[:, :128],
        small[:, 128:at],
        small[:, at],
        small[:, at + 2 : at + 2 + states],
        small[:, at + 1],
        out_shard.astype(F32),
        jnp.sqrt(out_sq / counted),
        jnp.sqrt(grad_sq / counted),
    )


def solution(mesh):
    dp, fsdp = mesh.devices.shape
    cores = 2 if fsdp % 2 == 0 else 1
    split = Mesh(mesh.devices.reshape(dp, fsdp // cores, cores), ALL)
    rows, flat, block = P(ALL, None), P(ALL), P(("fz", "core"), "dp")
    return jax.shard_map(
        per_device,
        mesh=split,
        in_specs=(
            rows, flat, flat, block, flat, block, rows, flat, rows, rows, flat, rows, flat, block, rows,
        ),
        out_specs=(
            rows, rows, block, flat, block, rows, flat, rows, rows, flat, rows, flat, block, P(), P(),
        ),
        check_vma=False,
    )
```

```python
import math

import jax
import jax.numpy as jnp
from jax import lax
from jax.experimental import pallas as pl
from jax.experimental.pallas import tpu as pltpu
from jax.sharding import Mesh, PartitionSpec as P

F32 = jnp.float32
BF16 = jnp.bfloat16
LN2 = math.log(2.0)
ALL = ("dp", "fz", "core")
high = lax.Precision.HIGHEST
GROUP = 4


def embed_columns(time_values, column, model_width):
    half_width = model_width // 2
    lower_half = column < half_width
    freq_index = jnp.where(lower_half, column, column - half_width).astype(F32)
    frequency = jnp.exp(freq_index * (-math.log(10000.0) / half_width))
    angles = time_values.astype(F32)[:, None] * frequency[None, :]
    return jax.nn.silu(jnp.where(lower_half[None, :], jnp.cos(angles), jnp.sin(angles)))


def fill_columns(proj_ref, bc_ref, tokens, first, group, states):
    def fill(i, _):
        p = proj_ref[pl.ds(pl.multiple_of(i * 8, 8), 8), :]
        for s in range(2):
            for n in range(GROUP):
                col = first + s * states + group * GROUP + n
                row = pl.multiple_of((s * GROUP + n) * tokens + i * 8, 8)
                bc_ref[pl.ds(row, 8), :] = jnp.broadcast_to(p[:, col : col + 1], (8, 128))
        return 0

    lax.fori_loop(0, tokens // 8, fill, 0, unroll=8)


VMEM = pl.BlockSpec(memory_space=pltpu.VMEM)
SMEM = pl.BlockSpec(memory_space=pltpu.SMEM)
ANY = pl.BlockSpec(memory_space=pl.ANY)


def dot(a, b):
    return jnp.dot(a, b, preferred_element_type=F32)


def dot_nt(a, b):
    return lax.dot_general(a, b, (((1,), (1,)), ((), ())), preferred_element_type=F32)


def shifted(ext, j, ahead):
    n = ext.shape[0] - 2
    sub = lax.broadcasted_iota(jnp.int32, (n, 8, 128), 1)
    if ahead:
        r = pltpu.roll(ext, 8 - j, 1)
        return jnp.where(sub >= 8 - j, r[2:], r[1:-1])
    r = pltpu.roll(ext, j, 1)
    return jnp.where(sub < j, r[:-2], r[1:-1])


def extended(ref, k, q, size, keep_ref, slots):
    zero = jnp.zeros((1, 8, 128), F32)
    lo, hi = q * size, (q + 1) * size
    before = ref[pl.ds(lo - 1, 1), k] * keep_ref[q] if q else zero
    after = ref[pl.ds(hi, 1), k] * keep_ref[q + 1] if q < slots - 1 else zero
    return jnp.concatenate([before, ref[pl.ds(lo, size), k], after], axis=0)


def convolved(ext, p, taps):
    here = ext[1:-1]
    both, moves = [], []
    for ahead in (False, True):
        c = p[taps : taps + 1][None] + p[taps - 1 : taps][None] * here
        for j in range(1, taps):
            m = shifted(ext, j, ahead)
            moves.append(m)
            c = c + p[taps - 1 - j : taps - j][None] * m
        both.append(c)
    return both, moves


def sublane_sums(vs):
    sub = lax.broadcasted_iota(jnp.int32, (8, 128), 0)
    for sh in (4, 2, 1):
        upper = (sub & sh) != 0
        half = len(vs) // 2
        vs = [
            jnp.where(
                upper,
                vs[q + half] + pltpu.roll(vs[q + half], sh, 0),
                vs[q] + pltpu.roll(vs[q], 8 - sh, 0),
            )
            for q in range(half)
        ]
    return vs[0]


def project(hidden, weight, *, rows, length, inner):
    blocks, owners, _, cols = weight.shape
    tiles = cols // 128

    def body(h_ref, w_ref, o_ref):
        w = w_ref[0].reshape(owners * rows, cols)
        r = dot(h_ref[...], w)
        for k in range(tiles):
            o_ref[:, k] = r[:, k * 128 : (k + 1) * 128].reshape(length // 8, 8, 128)

    return pl.pallas_call(
        body,
        grid=(blocks,),
        out_shape=jax.ShapeDtypeStruct((length // 8, inner // 128, 8, 128), F32),
        in_specs=[
            pl.BlockSpec(hidden.shape, lambda b: (0, 0)),
            pl.BlockSpec((1, owners, rows, cols), lambda b: (b, 0, 0, 0)),
        ],
        out_specs=pl.BlockSpec((length // 8, tiles, 8, 128), lambda b: (0, b, 0, 0)),
        compiler_params=pltpu.CompilerParams(vmem_limit_bytes=40 << 20),
        cost_estimate=pl.CostEstimate(
            flops=2 * length * hidden.shape[1] * inner,
            bytes_accessed=2 * hidden.shape[1] * inner + 4 * length * inner,
            transcendentals=0,
        ),
        name="project",
    )(hidden, weight)


def mixer_forward(keep, bound, x, x_proj, dt_proj, params, decay2, *, tokens, inner, states, rank, taps, slots):
    blocks, tiles, octets = inner // 1024, inner // 128, tokens // 8
    size = octets // slots
    rows = tokens * tiles

    def body(keep_ref, bound_ref, x_ref, xw_ref, dt_ref, p_ref, a_ref, y_ref, sf_ref, sr_ref, df_ref, dr_ref, proj_ref, bc_ref):
        shape4 = (octets, tiles, 8, 128)
        y4 = y_ref.reshape(shape4)
        s4 = (sf_ref.reshape(shape4), sr_ref.reshape(shape4))
        d4 = (df_ref.reshape(shape4), dr_ref.reshape(shape4))

        def conv(k, _):
            p = p_ref[k]
            skip = p[taps + 2 : taps + 3][None]
            for q in range(slots):
                both, _ = convolved(extended(x_ref, k, q, size, bound_ref, slots), p, taps)
                sl = pl.ds(q * size, size)
                series = [c * jax.nn.sigmoid(c) for c in both]
                for ref, v in zip(s4, series):
                    ref[sl, k] = v
                y4[sl, k] = skip * (series[0] + series[1])
            return 0

        lax.fori_loop(0, tiles, conv, 0)
        lanes = lax.broadcasted_iota(jnp.int32, (tokens, 128), 1)
        for s in range(2):
            total = jnp.zeros((tokens, 128), F32)
            for k in range(0, tiles, 2):
                lhs = jnp.concatenate(
                    [s4[s][:, k + i].reshape(tokens, 128).astype(BF16) for i in range(2)], axis=1
                )
                total = total + dot(lhs, xw_ref[pl.ds(k * 128, 256), :])
            proj_ref[s] = total
            low = jnp.where(lanes < rank, total, 0.0).astype(BF16)
            for k in range(0, tiles, 2):
                pre = dot_nt(low, dt_ref[pl.ds(k * 128, 256), :])
                for i in range(2):
                    v = pre[:, i * 128 : (i + 1) * 128] + p_ref[k + i, taps + 1 : taps + 2, :]
                    step = jnp.maximum(v, 0.0) + jnp.log1p(jnp.exp(-jnp.abs(v)))
                    d4[s][:, k + i] = step.reshape(octets, 8, 128)
        for s, (d_ref, u_ref) in enumerate(((df_ref, sf_ref), (dr_ref, sr_ref))):
            rev = s == 1
            for ng in range(states // GROUP):
                fill_columns(proj_ref.at[s], bc_ref, tokens, rank, ng, states)
                a = [
                    [a_ref[pl.ds((ng * GROUP + n) * tiles + c * 8, 8), :] for c in range(blocks)]
                    for n in range(GROUP)
                ]

                def octet(i, hs):
                    g = (octets - 1 - i) if rev else i
                    keep_now = keep_ref[s, i]
                    hs = [h * keep_now for h in hs]
                    base = pl.multiple_of(g * (tiles * 8), 8)
                    for j in range(8):
                        tt = 7 - j if rev else j
                        t = g * 8 + tt
                        for c in range(blocks):
                            sl = pl.ds(base + c * 64 + tt, 8, stride=8)
                            d = d_ref[sl, :]
                            du = d * u_ref[sl, :]
                            acc = None
                            for n in range(GROUP):
                                b = bc_ref[pl.ds(n * tokens + t, 1), :]
                                cc = bc_ref[pl.ds((GROUP + n) * tokens + t, 1), :]
                                k = n * blocks + c
                                hs[k] = jnp.exp2(d * a[n][c]) * hs[k] + du * b
                                acc = hs[k] * cc if acc is None else acc + hs[k] * cc
                            y_ref[sl, :] = y_ref[sl, :] + acc
                    return hs

                lax.fori_loop(0, octets, octet, [jnp.zeros((8, 128), F32)] * (GROUP * blocks))

    big = jax.ShapeDtypeStruct((rows, 128), F32)
    return pl.pallas_call(
        body,
        out_shape=(big,) * 5 + (jax.ShapeDtypeStruct((2, tokens, 128), F32),),
        in_specs=[SMEM, SMEM] + [VMEM] * 5,
        out_specs=(VMEM,) * 6,
        scratch_shapes=[pltpu.VMEM((2 * GROUP * tokens, 128), F32)],
        compiler_params=pltpu.CompilerParams(vmem_limit_bytes=56 << 20),
        cost_estimate=pl.CostEstimate(
            flops=tokens * inner * states * 160,
            bytes_accessed=6 * rows * 512,
            transcendentals=2 * tokens * inner * states,
        ),
        name="mixer_forward",
    )(keep, bound, x, x_proj, dt_proj, params, decay2)


def mixer_middle(place, hidden, weight, out_weight, branch_grad, total, *, rows, length, inner):
    blocks, owners, _, cols = weight.shape[0], weight.shape[1], 0, weight.shape[-1]
    packed = out_weight is None
    dp, per, wide = branch_grad.shape[0], owners // blocks, branch_grad.shape[2]
    tiles, octets = cols // 128, length // 8
    half = rows
    width = hidden.shape[1]

    def body(place_ref, h_ref, wz_ref, wo_ref, bg_ref, t_ref, g_ref, dz_ref, br_ref, *more):
        ml_ref, gz_ref, go_ref, ht_ref, sem = more[-5:]
        b = pl.program_id(0)
        where = place_ref[b]

        def copies():
            if packed:
                return [
                    pltpu.make_async_copy(gz_ref, more[0].at[b, :, 0], sem.at[0]),
                    pltpu.make_async_copy(go_ref, more[0].at[:, pl.ds(where * per, per), 1], sem.at[1]),
                ]
            return [
                pltpu.make_async_copy(gz_ref, more[0].at[b], sem.at[0]),
                pltpu.make_async_copy(go_ref, more[1].at[:, pl.ds(where * per, per)], sem.at[1]),
            ]

        z = dot(h_ref[...], wz_ref[...].reshape(owners * rows, cols))

        def out_rows(d):
            if not packed:
                return wo_ref[d].reshape(cols, wide)
            pieces = []
            for j in range(per):
                for i in range(2):
                    pieces.append(wo_ref[d, j, 0, :, i * wide : (i + 1) * wide])
            return jnp.concatenate(pieces, axis=0)

        mg = dot_nt(bg_ref[0], out_rows(0))
        for d in range(1, dp):
            mg = mg + dot_nt(bg_ref[d], out_rows(d))
        for k in range(tiles):
            sl = slice(k * 128, (k + 1) * 128)
            zk, mk, tk = z[:, sl], mg[:, sl], t_ref[:, k].reshape(length, 128)
            gate = jax.nn.sigmoid(zk)
            silu = zk * gate
            ml_ref[:, sl] = (tk * silu).astype(BF16)
            g_ref[:, k] = (mk * silu).reshape(octets, 8, 128)
            dz_ref[:, sl] = (mk * tk * (gate * (1.0 + zk * (1.0 - gate)))).astype(BF16)
        ml = ml_ref[...]
        ml_t = ml.T

        @pl.when(b == 0)
        def _():
            br_ref[...] = jnp.zeros_like(br_ref)
            ht_ref[...] = h_ref[...].T

        @pl.when(b > 0)
        def _():
            for c in copies():
                c.wait()

        for d in range(dp):
            br_ref[d] = br_ref[d] + dot(ml, out_rows(d))
            go = dot(ml_t, bg_ref[d]).astype(BF16)
            if packed:
                at = 0
                for j in range(per):
                    for i in range(2):
                        go_ref[d, j, :, i * wide : (i + 1) * wide] = go[at : at + half]
                        at += half
            else:
                go_ref[d] = go.reshape(go_ref.shape[1:])
        gz_ref[...] = dot(ht_ref[...], dz_ref[...]).astype(BF16).reshape(owners, rows, cols)
        for c in copies():
            c.start()

        @pl.when(b == blocks - 1)
        def _():
            for c in copies():
                c.wait()

    if packed:
        wz_spec = pl.BlockSpec((1, owners, 1, rows, cols), lambda b, p: (b, 0, 0, 0, 0))
        wo_spec = pl.BlockSpec((dp, per, 1, rows, cols), lambda b, p: (0, p[b], 1, 0, 0))
        extra = (jax.ShapeDtypeStruct((blocks, owners, 2, rows, cols), BF16),)
        go_shape = (dp, per, rows, cols)
        out_weight = weight
    else:
        wz_spec = pl.BlockSpec((1, owners, rows, cols), lambda b, p: (b, 0, 0, 0))
        wo_spec = pl.BlockSpec((dp, per, 2 * rows, wide), lambda b, p: (0, p[b], 0, 0))
        extra = (
            jax.ShapeDtypeStruct((blocks, owners, rows, cols), BF16),
            jax.ShapeDtypeStruct((dp, owners, 2 * rows, wide), BF16),
        )
        go_shape = (dp, per, 2 * rows, wide)
    whole = lambda v: pl.BlockSpec(v.shape, lambda b, p: (0,) * v.ndim)
    tile_spec = pl.BlockSpec((octets, tiles, 8, 128), lambda b, p: (0, b, 0, 0))
    return pl.pallas_call(
        body,
        grid_spec=pltpu.PrefetchScalarGridSpec(
            num_scalar_prefetch=1,
            grid=(blocks,),
            in_specs=[
                whole(hidden),
                wz_spec,
                wo_spec,
                whole(branch_grad),
                tile_spec,
            ],
            out_specs=(
                tile_spec,
                pl.BlockSpec((length, cols), lambda b, p: (0, b)),
                pl.BlockSpec((dp, length, wide), lambda b, p: (0, 0, 0)),
            )
            + (ANY,) * len(extra),
            scratch_shapes=[
                pltpu.VMEM((length, cols), BF16),
                pltpu.VMEM((owners, rows, cols), BF16),
                pltpu.VMEM(go_shape, BF16),
                pltpu.VMEM((width, length), BF16),
                pltpu.SemaphoreType.DMA((2,)),
            ],
        ),
        out_shape=(
            jax.ShapeDtypeStruct((octets, inner // 128, 8, 128), F32),
            jax.ShapeDtypeStruct((length, inner), BF16),
            jax.ShapeDtypeStruct((dp, length, wide), F32),
        )
        + extra,
        compiler_params=pltpu.CompilerParams(vmem_limit_bytes=56 << 20),
        cost_estimate=pl.CostEstimate(
            flops=10 * length * width * inner, bytes_accessed=60 << 20, transcendentals=length * inner
        ),
        name="mixer_middle",
    )(place, hidden, weight, out_weight, branch_grad, total)


def mixer_backward(keep, proj, step, series, grad, decay2, x_proj, dt_proj, params, *, rev, tokens, inner, states, rank, taps):
    blocks, tiles, octets = inner // 1024, inner // 128, tokens // 8
    slots = GROUP * blocks
    rows = tokens * tiles

    def body(
        keep_ref, proj_ref, d_ref, u_ref, g_ref, a_ref, xw_ref, dt_ref, p_ref,
        ddu_ref, small_ref, da_ref, skip_ref,
        dd_ref, bc_ref, h_ref, r_ref, cols_ref,
    ):
        zero = jnp.zeros((8, 128), F32)
        cols_ref[...] = jnp.zeros_like(cols_ref)
        for ng in range(states // GROUP):
            fill_columns(proj_ref, bc_ref, tokens, rank, ng, states)
            a = [
                [a_ref[pl.ds((ng * GROUP + n) * tiles + c * 8, 8), :] for c in range(blocks)]
                for n in range(GROUP)
            ]
            for k in range(slots):
                h_ref[pl.ds(k * 8, 8), :] = zero

            def ahead(i, hs):
                g = (octets - 1 - i) if rev else i
                keep_now = keep_ref[i]
                hs = [h * keep_now for h in hs]
                base = pl.multiple_of(g * (tiles * 8), 8)
                for j in range(8):
                    tt = 7 - j if rev else j
                    t = g * 8 + tt
                    hb = pl.multiple_of((i * 8 + j + 1) * (slots * 8), 8)
                    for c in range(blocks):
                        sl = pl.ds(base + c * 64 + tt, 8, stride=8)
                        d = d_ref[sl, :]
                        du = d * u_ref[sl, :]
                        for n in range(GROUP):
                            b = bc_ref[pl.ds(n * tokens + t, 1), :]
                            k = n * blocks + c
                            hs[k] = jnp.exp2(d * a[n][c]) * hs[k] + du * b
                            h_ref[pl.ds(hb + k * 8, 8), :] = hs[k]
                return hs

            lax.fori_loop(0, octets, ahead, [zero] * slots)

            def back(ii, carry):
                gs, das = [list(v) for v in carry]
                i = octets - 1 - ii
                g = (octets - 1 - i) if rev else i
                keep_now = keep_ref[i]
                base = pl.multiple_of(g * (tiles * 8), 8)
                for jj in range(8):
                    j = 7 - jj
                    tt = 7 - j if rev else j
                    t = g * 8 + tt
                    hb = pl.multiple_of((i * 8 + j) * (slots * 8), 8)
                    pb, pc = [None] * GROUP, [None] * GROUP
                    for c in range(blocks):
                        sl = pl.ds(base + c * 64 + tt, 8, stride=8)
                        d = d_ref[sl, :]
                        du = d * u_ref[sl, :]
                        gy = g_ref[sl, :]
                        ddu = dd = None
                        for n in range(GROUP):
                            b = bc_ref[pl.ds(n * tokens + t, 1), :]
                            cc = bc_ref[pl.ds((GROUP + n) * tokens + t, 1), :]
                            k = n * blocks + c
                            before = h_ref[pl.ds(hb + k * 8, 8), :]
                            after = h_ref[pl.ds(hb + (slots + k) * 8, 8), :]
                            adj = gs[k] + cc * gy
                            x = after * gy
                            pc[n] = x if c == 0 else pc[n] + x
                            x = adj * du
                            pb[n] = x if c == 0 else pb[n] + x
                            x = adj * b
                            ddu = x if n == 0 else ddu + x
                            moved = adj * jnp.exp2(d * a[n][c])
                            if j == 0:
                                moved = moved * keep_now
                            gs[k] = moved
                            m = moved * before
                            x = m * a[n][c]
                            dd = x if n == 0 else dd + x
                            das[k] = das[k] + m * d
                        if ng == 0:
                            ddu_ref[sl, :] = ddu
                            dd_ref[sl, :] = dd
                        else:
                            ddu_ref[sl, :] = ddu_ref[sl, :] + ddu
                            dd_ref[sl, :] = dd_ref[sl, :] + dd
                    r_ref[pl.ds(pl.multiple_of(t * 8, 8), 8), :] = sublane_sums(pb + pc)
                return gs, das

            _, das = lax.fori_loop(0, octets, back, ([zero] * slots, [zero] * slots))
            for n in range(GROUP):
                for c in range(blocks):
                    da_ref[pl.ds((ng * GROUP + n) * tiles + c * 8, 8), :] = das[n * blocks + c]
            lane = lax.broadcasted_iota(jnp.int32, (256, 128), 1)
            total = cols_ref[...]
            for q in range(2 * GROUP):
                col = rank + (q // GROUP) * states + ng * GROUP + q % GROUP
                one = jnp.where(lane == col, 1.0, 0.0).astype(BF16)
                v = r_ref[pl.ds(q, tokens, stride=8), :]
                high_part = v.astype(BF16)
                low_part = (v - high_part.astype(F32)).astype(BF16)
                total = total + dot(jnp.concatenate([high_part, low_part], axis=1), one)
            cols_ref[...] = total
        shape4 = (octets, tiles, 8, 128)
        d4, u4, g4, ddu4, dd4 = [r.reshape(shape4) for r in (d_ref, u_ref, g_ref, ddu_ref, dd_ref)]
        lanes = lax.broadcasted_iota(jnp.int32, (tokens, 128), 1)
        low = jnp.where(lanes < rank, proj_ref[...], jnp.where(lanes == rank, 1.0, 0.0)).astype(BF16)
        low_t = low.T
        proj_grad = jnp.zeros((tokens, 128), F32)
        for k in range(0, tiles, 2):
            pair = []
            for i in range(2):
                d, u, gy, ddu = d4[:, k + i], u4[:, k + i], g4[:, k + i], ddu4[:, k + i]
                pre = (ddu * u + LN2 * dd4[:, k + i]) * (1.0 - jnp.exp(-d))
                pair.append(pre.reshape(tokens, 128).astype(BF16))
                ddu4[:, k + i] = ddu * d + p_ref[k + i, taps + 2 : taps + 3, :][None] * gy
                skip_ref[k + i] = jnp.sum(gy * u, axis=0)
            pre = jnp.concatenate(pair, axis=1)
            proj_grad = proj_grad + dot(pre, dt_ref[pl.ds(k * 128, 256), :])
            small_ref[128:256, k * 128 : (k + 2) * 128] = dot(low_t, pre)
        proj_grad = jnp.where(lanes < rank, proj_grad, cols_ref[...]).astype(BF16)
        proj_t = proj_grad.T
        for k in range(0, tiles, 2):
            pair = [u4[:, k + i].reshape(tokens, 128).astype(BF16) for i in range(2)]
            small_ref[0:128, k * 128 : (k + 2) * 128] = dot(proj_t, jnp.concatenate(pair, axis=1))
            more = dot_nt(proj_grad, xw_ref[pl.ds(k * 128, 256), :])
            for i in range(2):
                ddu4[:, k + i] = ddu4[:, k + i] + more[:, i * 128 : (i + 1) * 128].reshape(octets, 8, 128)

    return pl.pallas_call(
        body,
        out_shape=(
            jax.ShapeDtypeStruct((rows, 128), F32),
            jax.ShapeDtypeStruct((256, inner), F32),
            jax.ShapeDtypeStruct((states * tiles, 128), F32),
            jax.ShapeDtypeStruct((tiles, 8, 128), F32),
        ),
        in_specs=[SMEM] + [VMEM] * 8,
        out_specs=(VMEM,) * 4,
        scratch_shapes=[
            pltpu.VMEM((rows, 128), F32),
            pltpu.VMEM((2 * GROUP * tokens, 128), F32),
            pltpu.VMEM((slots * 8 * (tokens + 1), 128), F32),
            pltpu.VMEM((tokens * 8, 128), F32),
            pltpu.VMEM((tokens, 128), F32),
        ],
        compiler_params=pltpu.CompilerParams(vmem_limit_bytes=60 << 20),
        cost_estimate=pl.CostEstimate(
            flops=tokens * inner * states * 160,
            bytes_accessed=5 * rows * 512,
            transcendentals=2 * tokens * inner * states,
        ),
        name="mixer_backward",
    )(keep, proj, step, series, grad, decay2, x_proj, dt_proj, params)


def mixer_finish(place, bound, x, grads, params, hidden, *, rows, cols, owners, length, inner, taps, slots):
    blocks = inner // cols
    tiles, octets = cols // 128, length // 8
    size = octets // slots
    width = hidden.shape[1]
    cores = 2
    fz = owners // cores

    def body(place_ref, bound_ref, x_ref, gf_ref, gr_ref, p_ref, h_ref, mine_ref, twin_ref, dx_ref, gw_ref, cf_ref, cr_ref, ht_ref):
        def first(k, _):
            p = p_ref[k]
            sums = [jnp.zeros((8, 128), F32) for _ in range(taps + 1)]
            for q in range(slots):
                ext = extended(x_ref, k, q, size, bound_ref, slots)
                both, moves = convolved(ext, p, taps)
                sl = pl.ds(q * size, size)
                for s, (c, src, dst) in enumerate(zip(both, (gf_ref, gr_ref), (cf_ref, cr_ref))):
                    gate = jax.nn.sigmoid(c)
                    dc = src[sl, k] * (gate * (1.0 + c * (1.0 - gate)))
                    dst[sl, k] = dc
                    sums[taps] = sums[taps] + jnp.sum(dc, axis=0)
                    sums[taps - 1] = sums[taps - 1] + jnp.sum(dc * ext[1:-1], axis=0)
                    for j in range(1, taps):
                        m = moves[s * (taps - 1) + j - 1]
                        sums[taps - 1 - j] = sums[taps - 1 - j] + jnp.sum(dc * m, axis=0)
            for i, v in enumerate(sums):
                gw_ref[k, i] = v
            return 0

        @pl.when(pl.program_id(0) == 0)
        def _():
            ht = h_ref[...].T
            for j in range(owners):
                at = ((j % cores) ^ place_ref[2]) * fz + ((j // cores) ^ place_ref[1])
                ht_ref[pl.ds(pl.multiple_of(at * rows, 16), rows), :] = ht[j * rows : (j + 1) * rows]

        lax.fori_loop(0, tiles, first, 0)
        for k in range(tiles):
            p = p_ref[k]
            for q in range(slots):
                ef = extended(cf_ref, k, q, size, bound_ref, slots)
                er = extended(cr_ref, k, q, size, bound_ref, slots)
                v = p[taps - 1 : taps][None] * (ef[1:-1] + er[1:-1])
                for j in range(1, taps):
                    v = v + p[taps - 1 - j : taps - j][None] * (shifted(ef, j, True) + shifted(er, j, False))
                dx_ref[pl.ds(q * size * 8, size * 8), k * 128 : (k + 1) * 128] = v.reshape(size * 8, 128).astype(BF16)
        dx = dx_ref[...]
        gx = dot(ht_ref[...], dx).astype(BF16).reshape(cores, fz, rows, cols)
        mine_ref[0] = gx[0]
        twin_ref[0] = gx[1]

    tile_spec = pl.BlockSpec((octets, tiles, 8, 128), lambda b, p: (0, b, 0, 0))
    part_spec = pl.BlockSpec((1, fz, rows, cols), lambda b, p: (b ^ p[0], 0, 0, 0))
    part = jax.ShapeDtypeStruct((blocks, fz, rows, cols), BF16)
    return pl.pallas_call(
        body,
        grid_spec=pltpu.PrefetchScalarGridSpec(
            num_scalar_prefetch=1,
            grid=(blocks,),
            in_specs=[
                SMEM,
                tile_spec,
                tile_spec,
                tile_spec,
                pl.BlockSpec((tiles, 8, 128), lambda b, p: (b, 0, 0)),
                pl.BlockSpec(hidden.shape, lambda b, p: (0, 0)),
            ],
            out_specs=(
                part_spec,
                part_spec,
                pl.BlockSpec((length, cols), lambda b, p: (0, b)),
                pl.BlockSpec((tiles, taps + 1, 8, 128), lambda b, p: (b, 0, 0, 0)),
            ),
            scratch_shapes=[
                pltpu.VMEM((octets, tiles, 8, 128), F32),
                pltpu.VMEM((octets, tiles, 8, 128), F32),
                pltpu.VMEM((width, length), BF16),
            ],
        ),
        out_shape=(
            part,
            part,
            jax.ShapeDtypeStruct((length, inner), BF16),
            jax.ShapeDtypeStruct((inner // 128, taps + 1, 8, 128), F32),
        ),
        compiler_params=pltpu.CompilerParams(vmem_limit_bytes=56 << 20),
        cost_estimate=pl.CostEstimate(
            flops=2 * length * width * inner, bytes_accessed=30 << 20, transcendentals=2 * length * inner
        ),
        name="mixer_finish",
    )(place, bound, x, grads[0], grads[1], params, hidden)


def hidden_back(x_grad, z_grad, wx, wz, *, rows):
    blocks, owners, cols = wx.shape[0], wx.shape[1], wx.shape[-1]
    length, width = x_grad.shape[0], owners * rows

    def body(dx_ref, dz_ref, wx_ref, wz_ref, hg_ref):
        hg = dot_nt(dx_ref[...], wx_ref[...].reshape(width, cols)) + dot_nt(
            dz_ref[...], wz_ref[...].reshape(width, cols)
        )

        @pl.when(pl.program_id(0) == 0)
        def _():
            hg_ref[...] = hg

        @pl.when(pl.program_id(0) > 0)
        def _():
            hg_ref[...] = hg_ref[...] + hg

    w_spec = pl.BlockSpec((1, owners, rows, cols), lambda b: (b, 0, 0, 0))
    z_spec = pl.BlockSpec((1, owners, 1, rows, cols), lambda b: (b, 0, 0, 0, 0)) if wz.ndim == 5 else w_spec
    return pl.pallas_call(
        body,
        grid=(blocks,),
        in_specs=[pl.BlockSpec((length, cols), lambda b: (0, b))] * 2 + [w_spec, z_spec],
        out_specs=pl.BlockSpec((length, width), lambda b: (0, 0)),
        out_shape=jax.ShapeDtypeStruct((length, width), F32),
        compiler_params=pltpu.CompilerParams(vmem_limit_bytes=40 << 20),
        cost_estimate=pl.CostEstimate(
            flops=4 * length * width * blocks * cols, bytes_accessed=24 << 20, transcendentals=0
        ),
        name="hidden_back",
    )(x_grad, z_grad, wx, wz)


def swap(v, axis, k):
    return lax.ppermute(v, axis, [(i, i ^ k) for i in range(lax.axis_size(axis))])


def others(v, axis):
    return jnp.stack([v] + [swap(v, axis, k) for k in range(1, lax.axis_size(axis))])


def gather_all(v):
    return others(others(others(v, "fz"), "dp"), "core")


def added(v, axis, dim):
    parts = [lax.index_in_dim(v, k, dim, keepdims=False) for k in range(lax.axis_size(axis))]
    return sum((swap(p, axis, k) if k else p).astype(F32) for k, p in enumerate(parts))


def relative(v, dim, me):
    n = v.shape[dim]
    return jnp.concatenate([lax.dynamic_slice_in_dim(v, me ^ k, 1, axis=dim) for k in range(n)], axis=dim)


def per_device(
    tokens,
    segment,
    timestep,
    ada_weight,
    ada_bias,
    in_weight,
    conv_weight,
    convolution_bias,
    xproj_weight,
    dtproj_weight,
    dt_bias,
    a_log,
    d_skip,
    out_weight,
    cotangent,
):
    dp, fz, cores = [lax.axis_size(n) for n in ALL]
    my_dp = lax.axis_index("dp")
    my_j = lax.axis_index("fz") * cores + lax.axis_index("core")
    fsdp = fz * cores
    devices = dp * fsdp
    slots = timestep.shape[0]
    length, width = tokens.shape
    taps, rank, states = conv_weight.shape[1], dtproj_weight.shape[1], a_log.shape[1]
    own = conv_weight.shape[0]
    inner = own * devices
    rows, cols = in_weight.shape[0], in_weight.shape[1] // 2
    wide = out_weight.shape[1]
    packs = wide % 128 == 0
    contract_rows = (((0,), (0,)), ((), ()))

    lower = my_dp < dp // 2
    opposite = [(i, (i + dp // 2) % dp) for i in range(dp)]
    left, right = in_weight[:, :cols], in_weight[:, cols:]
    got = lax.ppermute(jnp.where(lower, right, left), "dp", opposite)
    kept = jnp.where(lower, left, right)
    x_cols, z_cols = jnp.where(lower, kept, got), jnp.where(lower, got, kept)
    order = [(b % (dp // 2)) * 2 + b // (dp // 2) for b in range(dp)]

    parts = [
        xproj_weight,
        dtproj_weight,
        conv_weight,
        convolution_bias[:, None],
        dt_bias[:, None],
        d_skip[:, None],
        a_log,
    ]
    packed = jnp.concatenate(parts, axis=1)
    packed = jnp.pad(packed, ((0, 0), (0, 256 - packed.shape[1])))
    tail = own * 256 // cols
    g_x = lax.all_gather(jnp.concatenate([x_cols, packed.reshape(tail, cols)], axis=0), ALL, axis=0, tiled=True)
    g_x = g_x.reshape(dp, fsdp, rows + tail, cols)
    times = gather_all(timestep).reshape(-1)
    ada_rows, ada_cols = ada_weight.shape
    condition = embed_columns(
        times, my_j * ada_rows + jnp.arange(ada_rows, dtype=jnp.int32), width
    ).astype(BF16)
    bias_cols = ada_bias.shape[0]
    bias_part = lax.dynamic_update_slice(
        jnp.zeros((ada_cols,), F32), ada_bias.astype(F32), (my_j * bias_cols,)
    )
    partial = jnp.dot(condition, ada_weight, preferred_element_type=F32) + bias_part[None, :]
    partial = partial.reshape(cores, dp, fz, slots, ada_cols)
    partial = partial[0] + swap(partial[1], "core", 1)
    partial = partial[:, 0] + sum(swap(partial[:, k], "fz", k) for k in range(1, fz))
    blocks = jnp.stack([partial[0]] + [swap(partial[k], "dp", k) for k in range(1, dp)])
    modulation = jnp.concatenate(
        [lax.dynamic_index_in_dim(blocks, my_dp ^ b, keepdims=False) for b in range(dp)], axis=1
    )
    picker = (segment[:, None] == jnp.arange(slots, dtype=jnp.int32)[None, :]).astype(F32)
    per_token = jnp.dot(picker, modulation, precision=high)
    shift_mod = per_token[:, :width]
    scale_mod = per_token[:, width : 2 * width]
    gate_mod = per_token[:, 2 * width :]
    centered = tokens - jnp.mean(tokens, axis=1, keepdims=True)
    inv_std = lax.rsqrt(jnp.mean(centered * centered, axis=1, keepdims=True) + 1e-06)
    normed = centered * inv_std
    hidden = (normed * (1.0 + scale_mod) + shift_mod).astype(BF16)
    branch_grad = (cotangent * gate_mod).astype(BF16)
    branch_grad = branch_grad.reshape(length, dp, wide).transpose(1, 0, 2)

    if packs:
        out_piece = jnp.concatenate([out_weight[:rows], out_weight[rows:]], axis=1)
        later = jnp.stack([z_cols, out_piece])
        later, g_x, hidden = lax.optimization_barrier((later, g_x, hidden))
        g_z = lax.all_gather(later, ALL, axis=0, tiled=True).reshape(dp, fsdp, 2, rows, cols)
        g_out = None
    else:
        g_z = lax.all_gather(z_cols, ALL, axis=0, tiled=True).reshape(dp, fsdp, rows, cols)
        g_out = lax.all_gather(out_weight, ALL, axis=0, tiled=True).reshape(dp, fsdp, 2 * rows, wide)

    packed = g_x[:, :, rows:, :].reshape(dp, inner // dp, 256)
    packed = jnp.concatenate([packed[o] for o in order], axis=0)
    x_proj, dt_proj = packed[:, :128], packed[:, 128:256]
    rest = packed[:, 128 + rank :].astype(F32).T
    params = rest[:8].reshape(8, inner // 128, 128).transpose(1, 0, 2)
    decay = -jnp.exp(rest[taps + 3 : taps + 3 + states])
    decay2 = (decay * (1.0 / LN2)).reshape(states * inner // 128, 128)

    same = (segment[1:] == segment[:-1]).astype(F32)
    same = jnp.concatenate([jnp.zeros((1,), F32), same, jnp.zeros((1,), F32)])
    keep_f, keep_r = same[0:length:8], same[8 : length + 1 : 8][::-1]
    bound = same[0 : length : length // slots]
    sizes = dict(tokens=length, inner=inner, states=states, rank=rank, taps=taps)

    x = project(hidden, g_x, rows=rows, length=length, inner=inner)
    total, series_f, series_r, step_f, step_r, proj = mixer_forward(
        jnp.stack([keep_f, keep_r]), bound, x, x_proj, dt_proj, params, decay2, slots=slots, **sizes
    )
    tile_shape = (length // 8, inner // 128, 8, 128)
    middle = mixer_middle(
        jnp.asarray(order, jnp.int32),
        hidden,
        g_z,
        g_out,
        branch_grad,
        total.reshape(tile_shape),
        rows=rows,
        length=length,
        inner=inner,
    )
    grad, z_grad, branch = middle[:3]
    branch = branch.transpose(1, 0, 2).reshape(length, width)
    layer_out = tokens + gate_mod * branch
    gate_grad = cotangent * branch

    def scattered(v):
        return lax.psum_scatter(v.reshape(-1, v.shape[-1]), ALL, scatter_dimension=0, tiled=True)

    if packs:
        early = scattered(middle[3])
        z_shard, out_shard = early[:rows], early[rows:]
        out_shard = jnp.concatenate([out_shard[:, :wide], out_shard[:, wide:]], axis=0)
    else:
        z_shard, out_shard = early = scattered(middle[3]), scattered(middle[4])

    grad = grad.reshape(total.shape)
    series_grad, small, da, skip_part = [], 0.0, 0.0, 0.0
    for k, (keep, step, series) in enumerate(((keep_f, step_f, series_f), (keep_r, step_r, series_r))):
        got = mixer_backward(
            keep, proj[k], step, series, grad, decay2, x_proj, dt_proj, params, rev=k == 1, **sizes
        )
        series_grad.append(got[0].reshape(tile_shape))
        small, da, skip_part = small + got[1], da + got[2], skip_part + got[3]

    my_place = jnp.stack([lax.axis_index(n) for n in ALL]).astype(jnp.int32)
    mine, twin, x_grad, conv_part = mixer_finish(
        my_place,
        bound,
        x,
        series_grad,
        params,
        hidden,
        rows=rows,
        cols=cols,
        owners=fsdp,
        length=length,
        inner=inner,
        taps=taps,
        slots=slots,
    )
    small_t = jnp.concatenate(
        [
            small[: 128 + rank + 1],
            skip_part.sum(axis=1).reshape(1, inner),
            da.reshape(states, inner) * decay,
            jnp.zeros((256 - 128 - rank - 2 - states, inner), F32),
        ],
        axis=0,
    ).astype(BF16)
    small = small_t.T.reshape(dp, inner // dp, 256)
    small = jnp.concatenate([small[order.index(o)] for o in range(dp)], axis=0)
    small = small.reshape(dp, fz, cores, tail, cols)
    for dim, axis in enumerate(ALL):
        small = relative(small, dim, lax.axis_index(axis))
    small_twin = swap(small[:, :, 1], "core", 1)
    other = swap(twin, "core", 1)

    def both(k):
        a = mine[k].astype(F32) + other[k].astype(F32)
        return jnp.concatenate([a, small[k, :, 0].astype(F32) + small_twin[k].astype(F32)], axis=1)

    sends = [both(k).astype(BF16) for k in range(1, dp)]
    sends, x_grad, _ = lax.optimization_barrier((sends, x_grad, early))
    arrived = [swap(v, "dp", k + 1) for k, v in enumerate(sends)]
    arrived[0], x_grad = lax.optimization_barrier((arrived[0], x_grad))
    half_way = (both(0) + sum(v.astype(F32) for v in arrived)).astype(BF16)
    hidden_grad = hidden_back(x_grad, z_grad, g_x, g_z, rows=rows)

    normed_grad = hidden_grad * (1.0 + scale_mod)
    grad_tokens = cotangent + inv_std * (
        normed_grad
        - jnp.mean(normed_grad, axis=1, keepdims=True)
        - normed * jnp.mean(normed_grad * normed, axis=1, keepdims=True)
    )
    token_mod_grad = jnp.concatenate([hidden_grad, hidden_grad * normed, gate_grad], axis=1)
    mod_low = lax.dot_general(picker, token_mod_grad, contract_rows, precision=high).astype(BF16)
    valid = (segment < slots).astype(F32)[:, None]
    sums = jnp.stack(
        [
            jnp.sum(layer_out * layer_out * valid),
            jnp.sum(grad_tokens * grad_tokens * valid),
            jnp.sum(valid) * width,
        ]
    )
    pieces, rest = [], sums
    for _ in range(3):
        pieces.append(lax.optimization_barrier(rest.astype(BF16)))
        rest = rest - pieces[-1].astype(F32)
    pieces = jnp.pad(jnp.concatenate(pieces)[None, :], ((0, slots - 1), (0, 128 - 9)))
    conv_rows = conv_part.sum(axis=2).transpose(1, 0, 2).reshape((taps + 1) * inner)
    conv_cols = -(-conv_rows.shape[0] // (slots * 128)) * 128
    conv_rows = jnp.pad(conv_rows, (0, slots * conv_cols - conv_rows.shape[0]))
    mod_low = jnp.concatenate([mod_low, pieces, conv_rows.reshape(slots, conv_cols).astype(BF16)], axis=1)
    base = dp * ada_cols
    near = others(mod_low, "fz")
    conv_sum = near[:, :, base + 128 :].astype(F32).sum(axis=0).reshape(-1)[: (taps + 1) * inner]
    conv_sum = conv_sum.reshape(taps + 1, dp, inner // dp)
    conv_sum = jnp.stack([conv_sum[:, order.index(o)] for o in range(dp)]).reshape(dp, -1)
    conv_cols = -(-conv_sum.shape[1] // (fz * slots * 128)) * 128
    conv_sum = jnp.pad(conv_sum, ((0, 0), (0, fz * slots * conv_cols - conv_sum.shape[1]))).astype(BF16)
    conv_sum = conv_sum.reshape(dp, fz, slots, conv_cols)

    def part(k):
        return jnp.concatenate(
            [
                lax.dynamic_slice_in_dim(near, (my_dp ^ k) * ada_cols, ada_cols, axis=2),
                near[:, :, base : base + 128],
                lax.dynamic_index_in_dim(conv_sum, my_dp ^ k, keepdims=False),
            ],
            axis=2,
        )

    near = jnp.stack([part(0)] + [swap(part(k), "dp", k) for k in range(1, dp)])
    near = near.reshape(dp * fz * slots, -1)
    sides = (near, swap(near, "core", 1))
    conditions = condition.reshape(cores, dp * fz * slots, ada_rows)
    grad_ada_w, grad_ada_b, sums, conv_grad = 0.0, 0.0, 0.0, 0.0
    for side, cond in zip(sides, conditions):
        mod_cols = side[:, :ada_cols]
        grad_ada_w += lax.dot_general(cond, mod_cols, contract_rows, preferred_element_type=F32)
        mine_cols = lax.dynamic_slice_in_dim(mod_cols, my_j * bias_cols, bias_cols, axis=1)
        grad_ada_b += jnp.sum(mine_cols.astype(F32), axis=0)
        sums += jnp.sum(side[:, ada_cols : ada_cols + 9].astype(F32), axis=0)
        conv_grad += side[:, ada_cols + 128 :].astype(F32).reshape(dp, -1).sum(axis=0)
    conv_grad = conv_grad[: (taps + 1) * inner // dp].reshape(taps + 1, inner // dp)
    conv_grad = lax.dynamic_slice_in_dim(conv_grad, my_j * own, own, axis=1).T
    out_sq, grad_sq, counted = [sums[i] + sums[i + 3] + sums[i + 6] for i in range(3)]
    half_way = added(half_way, "fz", 0)
    small = half_way[rows:].reshape(own, 256)
    x_shard = half_way[:rows].astype(BF16)
    got = lax.ppermute(jnp.where(lower, z_shard, x_shard), "dp", opposite)
    grad_in_shard = jnp.where(
        lower,
        jnp.concatenate([x_shard, got], axis=1),
        jnp.concatenate([got, z_shard], axis=1),
    ).astype(F32)
    at = 128 + rank
    return (
        layer_out,
        grad_tokens,
        grad_ada_w,
        grad_ada_b,
        grad_in_shard,
        conv_grad[:, :taps],
        conv_grad[:, taps],
        small[:, :128],
        small[:, 128:at],
        small[:, at],
        small[:, at + 2 : at + 2 + states],
        small[:, at + 1],
        out_shard.astype(F32),
        jnp.sqrt(out_sq / counted),
        jnp.sqrt(grad_sq / counted),
    )


def solution(mesh):
    dp, fsdp = mesh.devices.shape
    cores = 2 if fsdp % 2 == 0 else 1
    split = Mesh(mesh.devices.reshape(dp, fsdp // cores, cores), ALL)
    rows, flat, block = P(ALL, None), P(ALL), P(("fz", "core"), "dp")
    return jax.shard_map(
        per_device,
        mesh=split,
        in_specs=(
            rows, flat, flat, block, flat, block, rows, flat, rows, rows, flat, rows, flat, block, rows,
        ),
        out_specs=(
            rows, rows, block, flat, block, rows, flat, rows, rows, flat, rows, flat, block, P(), P(),
        ),
        check_vma=False,
    )
```
